512 devices in a mesh: fsdp: 32 (over y_lo, z), tp: 16 (over y_hi, x, core).
Axes of the slice: x: 4, y: 4 (y_hi: 2, y_lo: 2; y = y_hi * 2 + y_lo), z: 16, core: 2. Of those that a mesh axis runs over, the one named last changes fastest.
Arguments:
- tokens: bfloat16 [4096, 4096], P('fsdp', 'tp'), may hold values from -6 to 6
- base_weight: bfloat16 [1, 4096, 4096], P(None, None, 'tp'), may hold values from -0.09375 to 0.09375
- a_old: bfloat16 [1, 128, 4096], P(None, 'fsdp'), may hold values from -0.09375 to 0.09375
- a_new: bfloat16 [1, 128, 4096], P(None, 'fsdp'), may hold values from -0.09375 to 0.09375
- b_old: bfloat16 [1, 4096, 128], P(None, 'fsdp'), may hold values from -0.5 to 0.5
- b_new: bfloat16 [1, 4096, 128], P(None, 'fsdp'), may hold values from -0.5 to 0.5
- gains: float32 [1, 4096], replicated, may hold values from 0.5 to 1.5
Outputs:
- stream_out: bfloat16 [4, 4096, 4096], P(None, 'fsdp', 'tp')
- merged: bfloat16 [1, 4096, 4096], P(None, None, 'tp')
The draws below stay inside these ranges and needn't reach their ends.
All inputs are finite; a program needn't handle non-finite values.
Results may differ from the reference program's by a relative error of at most 0.0069.
Values may be sent and summed in bfloat16 or wider, within the bound.
No kernel may reach another device: no remote copies, remote signals or barrier semaphores. Data moves between devices by JAX's collectives and lax.ppermute only.
A program may use at most 64 MiB of HBM per device.

```python
import jax
import jax.numpy as jnp
from jax import lax

D = 4096
RANK = 128
LAYERS = 1
STEPS = 4
ALL_ROWS = 4096


def block_scale(stream_key, shape, shards, least, top_value):
    gain, own = 1.0, jax.random.fold_in(stream_key, 6)
    for dim, blocks in shards:
        heights = jnp.exp(jax.random.uniform(jax.random.fold_in(own, dim), (blocks,), jnp.float32, least / len(shards), top_value / len(shards)))
        gain = gain * jnp.repeat(heights, shape[dim] // blocks).reshape([-1 if axis == dim else 1 for axis in range(len(shape))])
    return gain


def bell_draw(key, shape, deviation, most, split=(), kind=jnp.bfloat16):
    drawn = deviation * jax.random.normal(key, shape, jnp.float32)
    if split:
        drawn = drawn * block_scale(key, shape, split, -0.22, 0.18)
    return jnp.clip(drawn, -most, most).astype(kind)


def setup_inputs(seed: int = 0) -> dict:
    streams_of = jax.random.split(jax.random.key(seed), 8)
    tokens = bell_draw(streams_of[0], (ALL_ROWS, D), 1.0, 6.0, ((0, 32), (1, 16)))
    base_weight = bell_draw(streams_of[1], (LAYERS, D, D), D ** -0.5, 0.09375, ((2, 16),))
    a_old = bell_draw(streams_of[2], (LAYERS, RANK, D), D ** -0.5, 0.09375, ((1, 32),))
    a_new = bell_draw(streams_of[3], (LAYERS, RANK, D), D ** -0.5, 0.09375, ((1, 32),))
    b_old = bell_draw(streams_of[4], (LAYERS, D, RANK), RANK ** -0.5, 0.5, ((1, 32),))
    b_new = bell_draw(streams_of[5], (LAYERS, D, RANK), RANK ** -0.5, 0.5, ((1, 32),))
    gains = jnp.clip(1.0 + 0.1 * jax.random.normal(streams_of[6], (LAYERS, D), jnp.float32), 0.5, 1.5)
    return dict(tokens=tokens, base_weight=base_weight, a_old=a_old, a_new=a_new, b_old=b_old, b_new=b_new, gains=gains)


def reference(tokens, base_weight, a_old, a_new, b_old, b_new, gains):
    merged_all = []
    for layer in range(LAYERS):
        fresh = jnp.dot(a_new[layer].T, b_new[layer].T, preferred_element_type=jnp.float32)
        stale = jnp.dot(a_old[layer].T, b_old[layer].T, preferred_element_type=jnp.float32)
        delta = fresh - stale
        merged_all.append((base_weight[layer].astype(jnp.float32) + delta).astype(jnp.bfloat16))
    stream = tokens
    results = []
    for step in range(STEPS):
        for layer in range(LAYERS):
            values = stream.astype(jnp.float32)
            scale = lax.rsqrt(lax.optimization_barrier(jnp.mean(values * values, axis=-1, keepdims=True)) + 1e-06)
            normed = (values * scale * gains[layer]).astype(jnp.bfloat16)
            branch = jnp.dot(normed, merged_all[layer], preferred_element_type=jnp.float32)
            stream = (values + branch).astype(jnp.bfloat16)
        results.append(stream)
    return (jnp.stack(results), jnp.stack(merged_all))
```

```python
import jax
import jax.numpy as jnp
from jax import lax
from jax.sharding import PartitionSpec as P

STEPS = 4
CHIPS = 8
GROUPS = [[2 * chip + core for chip in range(CHIPS)] for core in range(2)]
SWAP = [(i, i ^ 1) for i in range(2 * CHIPS)]


def spread(blocks):
    own = lax.all_to_all(blocks, "tp", 0, 0, axis_index_groups=GROUPS)
    return own, lax.ppermute(own, "tp", SWAP)


def shards(tokens, base_weight, a_old, a_new, b_old, b_new, gains):
    rows, cols = tokens.shape
    tp = lax.axis_size("tp")
    fsdp = lax.axis_size("fsdp")
    t = lax.axis_index("tp")
    core = lax.rem(t, 2)

    def ordered(own, other):
        even = jnp.where(core == 0, own, other)
        odd = jnp.where(core == 0, other, own)
        return jnp.stack([even, odd], 1)

    share = b_old.shape[1] // tp
    low = a_old.shape[1]
    pick_a = lambda a: lax.dynamic_slice_in_dim(a[0], t * cols, cols, 1)
    pick_b = lambda b: lax.dynamic_slice_in_dim(b[0], t * share, share, 0)
    up = jnp.concatenate([pick_b(b_new), pick_b(b_old)], 1)
    message = jnp.concatenate([pick_a(a_new), pick_a(a_old), up], 0)
    got = lax.all_to_all(jnp.broadcast_to(message[None], (fsdp,) + message.shape), "fsdp", 0, 0)
    down_new = got[:, :low].reshape(fsdp * low, cols)
    down_old = got[:, low : 2 * low].reshape(fsdp * low, cols)
    ups = got[:, 2 * low :].reshape(CHIPS, -1, cols)

    common = jnp.concatenate([tokens, down_new, down_old], 0)
    first = jnp.concatenate([jnp.broadcast_to(common[None], (CHIPS,) + common.shape), ups], 1)
    own, other = spread(first)
    down = ordered(own[:, rows : rows + 2 * fsdp * low], other[:, rows : rows + 2 * fsdp * low])
    down = down.reshape(tp, 2 * fsdp * low, cols)
    ups = ordered(own[:, rows + 2 * fsdp * low :], other[:, rows + 2 * fsdp * low :])
    ups = ups.reshape(CHIPS, 2, 2, 2, share, cols)
    ups = lax.dynamic_index_in_dim(ups, core, 2, keepdims=False)
    ups = ups.transpose(2, 0, 1, 3, 4).reshape(cols, cols)
    half = cols // 2
    ups = jnp.concatenate([ups[:, :half], -ups[:, half:]], 1)
    delta = lax.dot_general(down, ups, (((1,), (1,)), ((), ())), preferred_element_type=jnp.float32)
    merged = (base_weight[0].astype(jnp.float32) + delta.reshape(tp * cols, cols)).astype(jnp.bfloat16)

    weights = merged.reshape(tp, cols, cols)
    gain = gains[0].reshape(tp, 1, cols)
    own, other = own[:, :rows], other[:, :rows]
    stream = tokens
    results = []
    for step in range(STEPS):
        if step:
            own, other = spread(jnp.broadcast_to(stream[None], (CHIPS,) + stream.shape))
        whole = ordered(own, other).reshape(tp, rows, cols).astype(jnp.float32)
        mean = jnp.sum(whole * whole, axis=(0, 2)) / (tp * cols)
        scale = lax.rsqrt(mean + 1e-06)[None, :, None]
        normed = (whole * scale * gain).astype(jnp.bfloat16)
        branch = lax.dot_general(
            normed.transpose(1, 0, 2).reshape(rows, tp * cols),
            merged,
            (((1,), (0,)), ((), ())),
            preferred_element_type=jnp.float32,
        )
        stream = (stream.astype(jnp.float32) + branch).astype(jnp.bfloat16)
        results.append(stream)
    return jnp.stack(results), merged[None]


def solution(mesh):
    placed = (
        P("fsdp", "tp"),
        P(None, None, "tp"),
        P(None, "fsdp", None),
        P(None, "fsdp", None),
        P(None, "fsdp", None),
        P(None, "fsdp", None),
        P(),
    )
    return jax.shard_map(
        shards,
        mesh=mesh,
        in_specs=placed,
        out_specs=(P(None, "fsdp", "tp"), P(None, None, "tp")),
        check_vma=False,
    )
```

```python
import jax
import jax.numpy as jnp
from jax import lax
from jax.experimental import pallas as pl
from jax.experimental.pallas import tpu as pltpu
from jax.sharding import PartitionSpec as P

STEPS = 4
CHIPS = 8
GROUPS = [[2 * chip + core for chip in range(CHIPS)] for core in range(2)]
PAIRS = [[2 * chip, 2 * chip + 1] for chip in range(CHIPS)]
SWAP = [(i, i ^ 1) for i in range(2 * CHIPS)]

VMEM = pl.BlockSpec(memory_space=pltpu.VMEM)
SMEM = pl.BlockSpec(memory_space=pltpu.SMEM)
ROOM = pltpu.CompilerParams(vmem_limit_bytes=24 * 1024 * 1024)


def spread(blocks):
    return lax.all_to_all(blocks, "tp", 0, 0, axis_index_groups=GROUPS)


def pack_kernel(got_ref, stream_ref, out_ref):
    fsdp, _, cols = got_ref.shape
    got = got_ref[...].astype(jnp.float32).reshape(fsdp, 2, 8, cols)
    down = got[:, 0].reshape(8 * fsdp, cols)
    came = lax.broadcasted_iota(jnp.int32, (8 * fsdp, cols), 0)
    goes = lax.broadcasted_iota(jnp.int32, (8 * fsdp, cols), 1)
    place = (came // 4 % 2) * (4 * fsdp) + came // 8 * 4 + came % 4
    order = jnp.where(place == goes, 1.0, 0.0).astype(jnp.bfloat16)
    down = jnp.dot(down.T.astype(jnp.bfloat16), order, preferred_element_type=jnp.float32).astype(jnp.bfloat16)
    stream = stream_ref[...].reshape(-1, cols)
    rows = stream.shape[0]
    each = fsdp // CHIPS
    for chip in range(CHIPS):
        out_ref[chip, :rows, :] = stream
        out_ref[chip, rows : rows + cols, :] = down
        ups = got[chip * each : (chip + 1) * each, 1].reshape(8 * each, cols)
        out_ref[chip, rows + cols :, :] = ups.astype(jnp.bfloat16)


def merge_kernel(core_ref, own_ref, other_ref, base_ref, mate_ref, weight_ref, merged_ref, up_ref):
    core = core_ref[0]
    cols = base_ref.shape[1]
    share = up_ref.shape[3]
    first = own_ref.shape[1] - cols - 4 * share
    for chip in range(CHIPS):
        for which, source in enumerate((own_ref, other_ref)):
            block = 2 * chip + (core if which == 0 else 1 - core)
            ups = source[chip, first + cols :, :].astype(jnp.float32).reshape(2, 2, share, cols)
            for j in range(2):
                up_ref[core, j, block] = ups[0, j]
                up_ref[1 - core, j, block] = ups[1, j]
    up = up_ref[...].reshape(2 * cols, cols).astype(jnp.bfloat16)
    for chip in range(CHIPS):
        for which, source in enumerate((own_ref, other_ref)):
            down = source[chip, first : first + cols, :]
            delta = lax.dot_general(down, up, (((1,), (1,)), ((), ())), preferred_element_type=jnp.float32)
            block = 2 * chip + (core if which == 0 else 1 - core)
            rows = pl.ds(pl.multiple_of(block * cols, cols), cols)
            mine = (base_ref[rows, :].astype(jnp.float32) + delta[:, :cols]).astype(jnp.bfloat16)
            merged_ref[rows, :] = mine
            weight_ref[2 * chip + which, :, :cols] = mine
            weight_ref[2 * chip + which, :, cols:] = (
                mate_ref[rows, :].astype(jnp.float32) + delta[:, cols:]
            ).astype(jnp.bfloat16)


def step_kernel(x_ref, weight_ref, gain_ref, mine_ref, out_ref):
    _, rows, cols = mine_ref.shape
    blocks = weight_ref.shape[0]
    part = lambda i: x_ref[i // 2, (i % 2) * rows : (i % 2 + 1) * rows, :].astype(jnp.float32)
    squares = part(0) * part(0)
    for i in range(1, blocks):
        squares += part(i) * part(i)
    mean = jnp.sum(squares, axis=1, keepdims=True) / (blocks * cols)
    scale = lax.rsqrt(mean + 1e-06)
    total = jnp.zeros((rows, 2 * cols), jnp.float32)
    for i in range(blocks):
        normed = (part(i) * scale * gain_ref[i]).astype(jnp.bfloat16)
        total += jnp.dot(normed, weight_ref[i], preferred_element_type=jnp.float32)
    for half in range(2):
        branch = total[:, half * cols : (half + 1) * cols]
        out_ref[half] = (mine_ref[half].astype(jnp.float32) + branch).astype(jnp.bfloat16)


def shards(tokens, base_weight, a_old, a_new, b_old, b_new, gains):
    rows, cols = tokens.shape
    tp = lax.axis_size("tp")
    fsdp = lax.axis_size("fsdp")
    t = lax.axis_index("tp")
    core = lax.rem(t, 2)
    half = rows // 2

    mate = lax.ppermute(base_weight[0], "tp", SWAP)
    both = lax.all_gather(tokens, "tp", axis=0, axis_index_groups=PAIRS)
    both = lax.dynamic_slice_in_dim(both, core * half, half, 1)
    stream = jnp.where(core == 0, both, both[::-1])

    share = b_old.shape[1] // tp
    low = a_old.shape[1]
    pick_a = lambda a: lax.dynamic_slice_in_dim(a[0], t * cols, cols, 1)
    pick_b = lambda b: lax.dynamic_slice_in_dim(b[0], t * share, share, 0)
    up = jnp.concatenate([pick_b(b_new), -pick_b(b_old)], 1)
    message = jnp.concatenate([pick_a(a_new), pick_a(a_old), up], 0)
    got = lax.all_to_all(jnp.broadcast_to(message[None], (fsdp,) + message.shape), "fsdp", 0, 0)
    packed = pl.pallas_call(
        pack_kernel,
        out_shape=jax.ShapeDtypeStruct((CHIPS, rows + cols + 4 * share, cols), jnp.bfloat16),
        in_specs=[VMEM] * 2,
        out_specs=VMEM,
        name="pack",
        compiler_params=ROOM,
    )(got, stream)
    packed, mate = lax.optimization_barrier((packed, mate))

    own = spread(packed)
    other = lax.ppermute(own, "tp", SWAP)
    weights, merged = pl.pallas_call(
        merge_kernel,
        out_shape=(
            jax.ShapeDtypeStruct((tp, cols, 2 * cols), jnp.bfloat16),
            jax.ShapeDtypeStruct((tp * cols, cols), jnp.bfloat16),
        ),
        in_specs=[SMEM] + [VMEM] * 4,
        out_specs=(VMEM, VMEM),
        scratch_shapes=[pltpu.VMEM((2, 2, tp, share, cols), jnp.float32)],
        name="merge",
        compiler_params=ROOM,
    )(core[None], own, other, base_weight[0], mate)

    gain = gains[0].reshape(CHIPS, 2, 1, cols)
    gain = jnp.where(core == 0, gain, gain[:, ::-1]).reshape(tp, 1, cols)
    x = own
    results = []
    for step in range(STEPS):
        if step:
            x = spread(jnp.broadcast_to(stream.reshape(1, rows, cols), (CHIPS, rows, cols)))
        stream = pl.pallas_call(
            step_kernel,
            out_shape=jax.ShapeDtypeStruct((2, half, cols), jnp.bfloat16),
            in_specs=[VMEM] * 4,
            out_specs=VMEM,
            name="step",
            compiler_params=ROOM,
        )(x, weights, gain, stream)
        results.append(stream)

    done = jnp.stack(results)
    swapped = lax.all_gather(done[:, 1], "tp", axis=0, axis_index_groups=PAIRS)
    swapped = lax.dynamic_index_in_dim(swapped, 1 - core, 0, keepdims=False)
    ends = jnp.stack([done[:, 0], swapped], 1)
    ends = jnp.where(core == 0, ends, ends[:, ::-1])
    return ends.reshape(STEPS, rows, cols), merged[None]


def solution(mesh):
    placed = (
        P("fsdp", "tp"),
        P(None, None, "tp"),
        P(None, "fsdp", None),
        P(None, "fsdp", None),
        P(None, "fsdp", None),
        P(None, "fsdp", None),
        P(),
    )
    return jax.shard_map(
        shards,
        mesh=mesh,
        in_specs=placed,
        out_specs=(P(None, "fsdp", "tp"), P(None, None, "tp")),
        check_vma=False,
    )
```

```python
import jax
import jax.numpy as jnp
from jax import lax
from jax.experimental import pallas as pl
from jax.experimental.pallas import tpu as pltpu
from jax.sharding import PartitionSpec as P

STEPS = 4
CHIPS = 8
GROUPS = [[2 * chip + core for chip in range(CHIPS)] for core in range(2)]
PAIRS = [[2 * chip, 2 * chip + 1] for chip in range(CHIPS)]
SWAP = [(i, i ^ 1) for i in range(2 * CHIPS)]
LINES = [[16 * low + z for z in range(16)] for low in range(2)]
RUNGS = [[z, 16 + z] for z in range(16)]

VMEM = pl.BlockSpec(memory_space=pltpu.VMEM)
SMEM = pl.BlockSpec(memory_space=pltpu.SMEM)
ROOM = pltpu.CompilerParams(vmem_limit_bytes=16 * 1024 * 1024)


def spread(blocks):
    return lax.all_to_all(blocks, "tp", 0, 0, axis_index_groups=GROUPS)


def pack_kernel(got_ref, stream_ref, out_ref):
    fsdp, _, cols = got_ref.shape
    got = got_ref[...].astype(jnp.float32).reshape(fsdp, 2, 8, cols)
    down = got[:, 0].reshape(8 * fsdp, cols)
    came = lax.broadcasted_iota(jnp.int32, (8 * fsdp, cols), 0)
    goes = lax.broadcasted_iota(jnp.int32, (8 * fsdp, cols), 1)
    place = (came // 4 % 2) * (4 * fsdp) + came // 8 * 4 + came % 4
    order = jnp.where(place == goes, 1.0, 0.0).astype(jnp.bfloat16)
    down = jnp.dot(down.T.astype(jnp.bfloat16), order, preferred_element_type=jnp.float32).astype(jnp.bfloat16)
    stream = stream_ref[...].reshape(-1, cols)
    rows = stream.shape[0]
    each = fsdp // CHIPS
    for chip in range(CHIPS):
        out_ref[chip, :rows, :] = stream
        out_ref[chip, rows : rows + cols, :] = down
        ups = got[chip * each : (chip + 1) * each, 1].reshape(8 * each, cols)
        out_ref[chip, rows + cols :, :] = ups.astype(jnp.bfloat16)


def merge_kernel(core_ref, own_ref, other_ref, base_ref, mate_ref, weight_ref, merged_ref, up_ref):
    core = core_ref[0]
    cols = base_ref.shape[1]
    share = up_ref.shape[3]
    first = own_ref.shape[1] - cols - 4 * share
    for chip in range(CHIPS):
        for which, source in enumerate((own_ref, other_ref)):
            block = 2 * chip + (core if which == 0 else 1 - core)
            ups = source[chip, first + cols :, :].astype(jnp.float32).reshape(2, 2, share, cols)
            for j in range(2):
                up_ref[core, j, block] = ups[0, j]
                up_ref[1 - core, j, block] = ups[1, j]
    up = up_ref[...].reshape(2 * cols, cols).astype(jnp.bfloat16)
    for chip in range(CHIPS):
        for which, source in enumerate((own_ref, other_ref)):
            down = source[chip, first : first + cols, :]
            delta = lax.dot_general(down, up, (((1,), (1,)), ((), ())), preferred_element_type=jnp.float32)
            block = 2 * chip + (core if which == 0 else 1 - core)
            rows = pl.ds(pl.multiple_of(block * cols, cols), cols)
            mine = (base_ref[rows, :].astype(jnp.float32) + delta[:, :cols]).astype(jnp.bfloat16)
            merged_ref[rows, :] = mine
            weight_ref[2 * chip + which, :, :cols] = mine
            weight_ref[2 * chip + which, :, cols:] = (
                mate_ref[rows, :].astype(jnp.float32) + delta[:, cols:]
            ).astype(jnp.bfloat16)


def step_kernel(x_ref, weight_ref, gain_ref, mine_ref, out_ref):
    _, rows, cols = mine_ref.shape
    blocks = weight_ref.shape[0]
    part = lambda i: x_ref[i // 2, (i % 2) * rows : (i % 2 + 1) * rows, :].astype(jnp.float32)
    squares = part(0) * part(0)
    for i in range(1, blocks):
        squares += part(i) * part(i)
    mean = jnp.sum(squares, axis=1, keepdims=True) / (blocks * cols)
    scale = lax.rsqrt(mean + 1e-06)
    total = jnp.zeros((rows, 2 * cols), jnp.float32)
    for i in range(blocks):
        normed = (part(i) * scale * gain_ref[i]).astype(jnp.bfloat16)
        total += jnp.dot(normed, weight_ref[i], preferred_element_type=jnp.float32)
    for half in range(2):
        branch = total[:, half * cols : (half + 1) * cols]
        out_ref[half] = (mine_ref[half].astype(jnp.float32) + branch).astype(jnp.bfloat16)


def finish_kernel(core_ref, swapped_ref, *refs):
    core = core_ref[0]
    out_ref = refs[-1]
    half = swapped_ref.shape[1]
    mine = pl.ds(pl.multiple_of(core * half, half), half)
    theirs = pl.ds(pl.multiple_of((1 - core) * half, half), half)
    for step in range(STEPS):
        out_ref[step, mine, :] = refs[step][0]
        out_ref[step, theirs, :] = swapped_ref[step]


def shards(tokens, base_weight, a_old, a_new, b_old, b_new, gains):
    rows, cols = tokens.shape
    tp = lax.axis_size("tp")
    fsdp = lax.axis_size("fsdp")
    t = lax.axis_index("tp")
    core = lax.rem(t, 2)
    half = rows // 2

    both = lax.all_gather(tokens, "tp", axis=0, axis_index_groups=PAIRS)
    both, base = lax.optimization_barrier((both, base_weight[0]))
    mate = lax.ppermute(base, "tp", SWAP)
    both = lax.dynamic_slice_in_dim(both, core * half, half, 1)
    stream = jnp.where(core == 0, both, both[::-1])

    share = b_old.shape[1] // tp
    low = a_old.shape[1]
    pick_a = lambda a: lax.dynamic_slice_in_dim(a[0], t * cols, cols, 1)
    pick_b = lambda b: lax.dynamic_slice_in_dim(b[0], t * share, share, 0)
    up = jnp.concatenate([pick_b(b_new), -pick_b(b_old)], 1)
    message = jnp.concatenate([pick_a(a_new), pick_a(a_old), up], 0)
    line = len(LINES[0])
    got = lax.all_to_all(
        jnp.broadcast_to(message[None], (line,) + message.shape), "fsdp", 0, 0, axis_index_groups=LINES
    )
    got = lax.all_gather(got, "fsdp", axis=0, tiled=True, axis_index_groups=RUNGS)
    packed = pl.pallas_call(
        pack_kernel,
        out_shape=jax.ShapeDtypeStruct((CHIPS, rows + cols + 4 * share, cols), jnp.bfloat16),
        in_specs=[VMEM] * 2,
        out_specs=VMEM,
        name="pack",
        compiler_params=ROOM,
    )(got, stream)
    packed, mate = lax.optimization_barrier((packed, mate))

    own = spread(packed)
    other = lax.ppermute(own, "tp", SWAP)
    weights, merged = pl.pallas_call(
        merge_kernel,
        out_shape=(
            jax.ShapeDtypeStruct((tp, cols, 2 * cols), jnp.bfloat16),
            jax.ShapeDtypeStruct((tp * cols, cols), jnp.bfloat16),
        ),
        in_specs=[SMEM] + [VMEM] * 4,
        out_specs=(VMEM, VMEM),
        scratch_shapes=[pltpu.VMEM((2, 2, tp, share, cols), jnp.float32)],
        name="merge",
        compiler_params=ROOM,
    )(core[None], own, other, base_weight[0], mate)

    gain = gains[0].reshape(CHIPS, 2, 1, cols)
    gain = jnp.where(core == 0, gain, gain[:, ::-1]).reshape(tp, 1, cols)
    x = own
    results = []
    for step in range(STEPS):
        if step:
            x = spread(jnp.broadcast_to(stream.reshape(1, rows, cols), (CHIPS, rows, cols)))
        stream = pl.pallas_call(
            step_kernel,
            out_shape=jax.ShapeDtypeStruct((2, half, cols), jnp.bfloat16),
            in_specs=[VMEM] * 4,
            out_specs=VMEM,
            name="step",
            compiler_params=ROOM,
        )(x, weights, gain, stream)
        results.append(stream)

    swapped = lax.ppermute(jnp.stack([result[1] for result in results]), "tp", SWAP)
    ends = pl.pallas_call(
        finish_kernel,
        out_shape=jax.ShapeDtypeStruct((STEPS, rows, cols), jnp.bfloat16),
        in_specs=[SMEM] + [VMEM] * (STEPS + 1),
        out_specs=VMEM,
        name="finish",
        compiler_params=ROOM,
    )(core[None], swapped, *results)
    return ends, merged[None]


def solution(mesh):
    placed = (
        P("fsdp", "tp"),
        P(None, None, "tp"),
        P(None, "fsdp", None),
        P(None, "fsdp", None),
        P(None, "fsdp", None),
        P(None, "fsdp", None),
        P(),
    )
    return jax.shard_map(
        shards,
        mesh=mesh,
        in_specs=placed,
        out_specs=(P(None, "fsdp", "tp"), P(None, None, "tp")),
        check_vma=False,
    )
```

```python
import jax
import jax.numpy as jnp
from jax import lax
from jax.experimental import pallas as pl
from jax.experimental.pallas import tpu as pltpu
from jax.sharding import PartitionSpec as P

STEPS = 4
CHIPS = 8
GROUPS = [[2 * chip + core for chip in range(CHIPS)] for core in range(2)]
PAIRS = [[2 * chip, 2 * chip + 1] for chip in range(CHIPS)]
SWAP = [(i, i ^ 1) for i in range(2 * CHIPS)]
PLANES = [
    [(16 * (y % 2) + z) * 16 + 8 * (y // 2) + 2 * x + core for y in range(4) for x in range(4)]
    for z in range(16)
    for core in range(2)
]
SHIFTED = [
    ((16 * low + z) * 16 + t, (16 * low + (z + t // 2 + 8 * (t % 2)) % 16) * 16 + t)
    for low in range(2)
    for z in range(16)
    for t in range(16)
]


def relay(part):
    pairs = []
    for z in range(16):
        for low in range(2):
            for block in range(16):
                shift = (z - block) % 16
                source = (16 * low + z) * 16 + 2 * (shift % 8) + shift // 8
                target = 16 * ((block % 4 // 2) ^ part) + z
                pairs.append((source, target * 16 + 8 * low + 2 * (block // 4) + block % 2))
    return pairs


VMEM = pl.BlockSpec(memory_space=pltpu.VMEM)
SMEM = pl.BlockSpec(memory_space=pltpu.SMEM)
ROOM = pltpu.CompilerParams(vmem_limit_bytes=16 * 1024 * 1024)


def spread(blocks):
    return lax.all_to_all(blocks, "tp", 0, 0, axis_index_groups=GROUPS)


def block_kernel(a_new_ref, a_old_ref, b_new_ref, b_old_ref, out_ref):
    half, cols = out_ref.shape[0] // 2, out_ref.shape[1]
    new = a_new_ref[0].astype(jnp.float32)
    old = a_old_ref[0].astype(jnp.float32)
    slices = []
    for i in range(new.shape[1] // cols):
        slices += [new[:, i * cols : (i + 1) * cols], old[:, i * cols : (i + 1) * cols]]
    out_ref[:half, :] = jnp.concatenate(slices, 0).astype(jnp.bfloat16)
    out_ref[half:, :] = jnp.concatenate([b_new_ref[0], -b_old_ref[0]], 1)


def merge_kernel(place_ref, own_ref, other_ref, ups_ref, base_ref, mate_ref, weight_ref, merged_ref, up_ref):
    core, low, z = place_ref[0], place_ref[1], place_ref[2]
    cols = base_ref.shape[1]
    for left in range(2):
        for part in range(2):
            up_ref[lax.rem(part + low + core, 2), left] = ups_ref[left, part]
    goes = lax.broadcasted_iota(jnp.int32, (cols, cols), 0)
    comes = lax.broadcasted_iota(jnp.int32, (cols, cols), 1)
    chip = comes // 8 % 16
    shift = chip // 8 * 4 + chip % 4 + 8 * ((comes // 128 + core) % 2)
    block = chip // 4 % 2 * 16 + (z + 32 - shift) % 16
    place = comes // 4 % 2 * 128 + block * 4 + comes % 4
    order = jnp.where(place == goes, 1.0, 0.0).astype(jnp.bfloat16)
    up = jnp.dot(up_ref[...].reshape(2 * cols, cols), order, preferred_element_type=jnp.float32).astype(jnp.bfloat16)
    for pair in range(CHIPS):
        parts = [
            ref[:, 16 * pair : 16 * pair + 16, :].astype(jnp.float32).reshape(16, 2, 8, cols)
            for ref in (own_ref, other_ref)
        ]
        for right in range(2):
            down = jnp.concatenate([part[:, right].reshape(128, cols) for part in parts], 0)
            down = down.T.astype(jnp.bfloat16)
            delta = lax.dot_general(down, up, (((1,), (1,)), ((), ())), preferred_element_type=jnp.float32)
            t = 2 * pair + right
            rows = slice(t * cols, (t + 1) * cols)
            mine = (base_ref[rows, :].astype(jnp.float32) + delta[:, :cols]).astype(jnp.bfloat16)
            theirs = (mate_ref[rows, :].astype(jnp.float32) + delta[:, cols:]).astype(jnp.bfloat16)
            merged_ref[rows, :] = mine
            which = 2 * pair + lax.rem(right + core, 2)
            weight_ref[which, :, :cols] = mine
            weight_ref[which, :, cols:] = theirs


def step_kernel(x_ref, weight_ref, gain_ref, mine_ref, out_ref, _):
    _, rows, cols = mine_ref.shape
    blocks = weight_ref.shape[0]
    part = lambda i: x_ref[i // 2, (i % 2) * rows : (i % 2 + 1) * rows, :].astype(jnp.float32)
    squares = part(0) * part(0)
    for i in range(1, blocks):
        squares += part(i) * part(i)
    mean = jnp.sum(squares, axis=1, keepdims=True) / (blocks * cols)
    scale = lax.rsqrt(mean + 1e-06)
    total = jnp.zeros((rows, 2 * cols), jnp.float32)
    for i in range(blocks):
        normed = (part(i) * scale * gain_ref[i]).astype(jnp.bfloat16)
        total += jnp.dot(normed, weight_ref[i], preferred_element_type=jnp.float32)
    for half in range(2):
        branch = total[:, half * cols : (half + 1) * cols]
        out_ref[half] = (mine_ref[half].astype(jnp.float32) + branch).astype(jnp.bfloat16)


def finish_kernel(core_ref, swapped_ref, *refs):
    core = core_ref[0]
    out_ref = refs[-1]
    half = swapped_ref.shape[1]
    mine = pl.ds(pl.multiple_of(core * half, half), half)
    theirs = pl.ds(pl.multiple_of((1 - core) * half, half), half)
    for step in range(STEPS):
        out_ref[step, mine, :] = refs[step][0]
        out_ref[step, theirs, :] = swapped_ref[step]


def shards(tokens, base_weight, a_old, a_new, b_old, b_new, gains):
    rows, cols = tokens.shape
    tp = lax.axis_size("tp")
    t = lax.axis_index("tp")
    core = lax.rem(t, 2)
    half = rows // 2

    block = pl.pallas_call(
        block_kernel,
        out_shape=jax.ShapeDtypeStruct((2 * b_old.shape[1], cols), jnp.bfloat16),
        in_specs=[VMEM] * 4,
        out_specs=VMEM,
        name="block",
        compiler_params=ROOM,
    )(a_new, a_old, b_new, b_old)
    block = lax.ppermute(block, ("fsdp", "tp"), SHIFTED)

    both = lax.all_gather(tokens, "tp", axis=0, axis_index_groups=PAIRS)
    both, base = lax.optimization_barrier((both, base_weight[0]))
    mate = lax.ppermute(base, "tp", SWAP)
    both = lax.dynamic_slice_in_dim(both, core * half, half, 1)
    stream = jnp.where(core == 0, both, both[::-1])
    x = spread(jnp.broadcast_to(stream.reshape(1, rows, cols), (CHIPS, rows, cols)))
    block, x = lax.optimization_barrier((block, x))

    down, up = block[: block.shape[0] // 2], block[block.shape[0] // 2 :]
    ups = [lax.ppermute(up, ("fsdp", "tp"), relay(part)) for part in range(2)]
    own = jnp.broadcast_to(down[None], (len(PLANES[0]),) + down.shape)
    own = lax.all_to_all(own, ("fsdp", "tp"), 0, 0, axis_index_groups=PLANES)
    own, *ups = lax.optimization_barrier((own, *ups))
    other = lax.ppermute(own, "tp", SWAP)
    ups = lax.all_gather(jnp.stack(ups), "tp", axis=0, axis_index_groups=PAIRS)
    f = lax.axis_index("fsdp")
    place = jnp.stack([core, f // 16, f % 16])
    weights, merged = pl.pallas_call(
        merge_kernel,
        out_shape=(
            jax.ShapeDtypeStruct((tp, cols, 2 * cols), jnp.bfloat16),
            jax.ShapeDtypeStruct((tp * cols, cols), jnp.bfloat16),
        ),
        in_specs=[SMEM] + [VMEM] * 5,
        out_specs=(VMEM, VMEM),
        scratch_shapes=[pltpu.VMEM((2, 2, cols // 2, cols), jnp.bfloat16)],
        name="merge",
        compiler_params=ROOM,
    )(place, own, other, ups, base_weight[0], mate)

    gain = gains[0].reshape(CHIPS, 2, 1, cols)
    gain = jnp.where(core == 0, gain, gain[:, ::-1]).reshape(tp, 1, cols)
    results = []
    for step in range(STEPS):
        if step:
            x = spread(jnp.broadcast_to(stream.reshape(1, rows, cols), (CHIPS, rows, cols)))
        stream, weights = pl.pallas_call(
            step_kernel,
            out_shape=(
                jax.ShapeDtypeStruct((2, half, cols), jnp.bfloat16),
                jax.ShapeDtypeStruct(weights.shape, weights.dtype),
            ),
            in_specs=[VMEM] * 4,
            out_specs=(VMEM, VMEM),
            input_output_aliases={1: 1},
            name="step",
            compiler_params=ROOM,
        )(x, weights, gain, stream)
        results.append(stream)

    swapped = lax.ppermute(jnp.stack([result[1] for result in results]), "tp", SWAP)
    ends = pl.pallas_call(
        finish_kernel,
        out_shape=jax.ShapeDtypeStruct((STEPS, rows, cols), jnp.bfloat16),
        in_specs=[SMEM] + [VMEM] * (STEPS + 1),
        out_specs=VMEM,
        name="finish",
        compiler_params=ROOM,
    )(core[None], swapped, *results)
    return ends, merged[None]


def solution(mesh):
    placed = (
        P("fsdp", "tp"),
        P(None, None, "tp"),
        P(None, "fsdp", None),
        P(None, "fsdp", None),
        P(None, "fsdp", None),
        P(None, "fsdp", None),
        P(),
    )
    return jax.shard_map(
        shards,
        mesh=mesh,
        in_specs=placed,
        out_specs=(P(None, "fsdp", "tp"), P(None, None, "tp")),
        check_vma=False,
    )
```

```python
import jax
import jax.numpy as jnp
from jax import lax
from jax.experimental import pallas as pl
from jax.experimental.pallas import tpu as pltpu
from jax.sharding import PartitionSpec as P

STEPS = 4
CHIPS = 8
GROUPS = [[2 * chip + core for chip in range(CHIPS)] for core in range(2)]
PAIRS = [[2 * chip, 2 * chip + 1] for chip in range(CHIPS)]
SWAP = [(i, i ^ 1) for i in range(2 * CHIPS)]
PLANES = [
    [(16 * (y % 2) + z) * 16 + 8 * (y // 2) + 2 * x + core for y in range(4) for x in range(4)]
    for z in range(16)
    for core in range(2)
]
SHIFTED = [
    ((16 * low + z) * 16 + t, (16 * low + (z + t // 2 + 8 * (t % 2)) % 16) * 16 + t)
    for low in range(2)
    for z in range(16)
    for t in range(16)
]


def relay(part):
    pairs = []
    for z in range(16):
        for low in range(2):
            for block in range(16):
                shift = (z - block) % 16
                source = (16 * low + z) * 16 + 2 * (shift % 8) + shift // 8
                target = 16 * ((block % 4 // 2) ^ part) + z
                pairs.append((source, target * 16 + 8 * low + 2 * (block // 4) + block % 2))
    return pairs


VMEM = pl.BlockSpec(memory_space=pltpu.VMEM)
SMEM = pl.BlockSpec(memory_space=pltpu.SMEM)
ANY = pl.BlockSpec(memory_space=pl.ANY)
ROOM = pltpu.CompilerParams(vmem_limit_bytes=16 * 1024 * 1024)


def spread(blocks):
    return lax.all_to_all(blocks, "tp", 0, 0, axis_index_groups=GROUPS)


def block_kernel(a_new_ref, a_old_ref, b_new_ref, b_old_ref, out_ref, a_ref, b_ref, sems):
    copies = [
        pltpu.make_async_copy(source, target, sems.at[i])
        for i, (source, target) in enumerate(
            ((a_new_ref, a_ref.at[0]), (a_old_ref, a_ref.at[1]), (b_new_ref, b_ref.at[0]), (b_old_ref, b_ref.at[1]))
        )
    ]
    for copy in copies:
        copy.start()
    for copy in copies:
        copy.wait()
    half, cols = out_ref.shape[0] // 2, out_ref.shape[1]
    new = a_ref[0, 0].astype(jnp.float32)
    old = a_ref[1, 0].astype(jnp.float32)
    slices = []
    for i in range(new.shape[1] // cols):
        slices += [new[:, i * cols : (i + 1) * cols], old[:, i * cols : (i + 1) * cols]]
    out_ref[:half, :] = jnp.concatenate(slices, 0).astype(jnp.bfloat16)
    out_ref[half:, :] = jnp.concatenate([b_ref[0, 0], -b_ref[1, 0]], 1)


def split_kernel(block_ref, down_ref, up_ref):
    half = up_ref.shape[0]
    for chip in range(down_ref.shape[0]):
        down_ref[chip] = block_ref[:half, :]
    up_ref[...] = block_ref[half:, :]


def merge_kernel(
    place_ref, own_ref, other_ref, ups_ref, base_ref, mate_ref, weight_ref, merged_ref, up_ref, old_ref, new_ref, in_sems, out_sems
):
    core, low, z = place_ref[0], place_ref[1], place_ref[2]
    cols = base_ref.shape[1]
    span = 2 * cols
    loads = []
    for pair in range(CHIPS):
        rows = slice(pair * span, (pair + 1) * span)
        loads.append(
            [
                pltpu.make_async_copy(ref.at[rows], old_ref.at[i, rows], in_sems.at[i, pair])
                for i, ref in enumerate((base_ref, mate_ref))
            ]
        )
        for load in loads[-1]:
            load.start()
    stores = []
    for left in range(2):
        for part in range(2):
            up_ref[lax.rem(part + low + core, 2), left] = ups_ref[left, part]
    goes = lax.broadcasted_iota(jnp.int32, (cols, cols), 0)
    comes = lax.broadcasted_iota(jnp.int32, (cols, cols), 1)
    chip = comes // 8 % 16
    shift = chip // 8 * 4 + chip % 4 + 8 * ((comes // 128 + core) % 2)
    block = chip // 4 % 2 * 16 + (z + 32 - shift) % 16
    place = comes // 4 % 2 * 128 + block * 4 + comes % 4
    order = jnp.where(place == goes, 1.0, 0.0).astype(jnp.bfloat16)
    up = jnp.dot(up_ref[...].reshape(2 * cols, cols), order, preferred_element_type=jnp.float32).astype(jnp.bfloat16)
    for pair in range(CHIPS):
        parts = [
            ref[:, 16 * pair : 16 * pair + 16, :].astype(jnp.float32).reshape(16, 2, 8, cols)
            for ref in (own_ref, other_ref)
        ]
        for load in loads[pair]:
            load.wait()
        for right in range(2):
            down = jnp.concatenate([part[:, right].reshape(128, cols) for part in parts], 0)
            down = down.T.astype(jnp.bfloat16)
            delta = lax.dot_general(down, up, (((1,), (1,)), ((), ())), preferred_element_type=jnp.float32)
            t = 2 * pair + right
            rows = slice(t * cols, (t + 1) * cols)
            mine = (old_ref[0, rows, :].astype(jnp.float32) + delta[:, :cols]).astype(jnp.bfloat16)
            theirs = (old_ref[1, rows, :].astype(jnp.float32) + delta[:, cols:]).astype(jnp.bfloat16)
            new_ref[rows, :] = mine
            which = 2 * pair + lax.rem(right + core, 2)
            weight_ref[which, :, :cols] = mine
            weight_ref[which, :, cols:] = theirs
        rows = slice(pair * span, (pair + 1) * span)
        stores.append(pltpu.make_async_copy(new_ref.at[rows], merged_ref.at[rows], out_sems.at[pair]))
        stores[-1].start()
    for store in stores:
        store.wait()


def step_kernel(x_ref, weight_ref, gain_ref, mine_ref, out_ref, give_ref, _):
    _, rows, cols = mine_ref.shape
    blocks = weight_ref.shape[0]
    part = lambda i: x_ref[i // 2, (i % 2) * rows : (i % 2 + 1) * rows, :].astype(jnp.float32)
    squares = part(0) * part(0)
    for i in range(1, blocks):
        squares += part(i) * part(i)
    mean = jnp.sum(squares, axis=1, keepdims=True) / (blocks * cols)
    scale = lax.rsqrt(mean + 1e-06)
    total = jnp.zeros((rows, 2 * cols), jnp.float32)
    for i in range(blocks):
        normed = (part(i) * scale * gain_ref[i]).astype(jnp.bfloat16)
        total += jnp.dot(normed, weight_ref[i], preferred_element_type=jnp.float32)
    for half in range(2):
        branch = total[:, half * cols : (half + 1) * cols]
        out_ref[half] = (mine_ref[half].astype(jnp.float32) + branch).astype(jnp.bfloat16)
    give_ref[...] = out_ref[1]


def finish_kernel(core_ref, swapped_ref, *refs):
    core = core_ref[0]
    out_ref = refs[-1]
    half = swapped_ref.shape[1]
    mine = pl.ds(pl.multiple_of(core * half, half), half)
    theirs = pl.ds(pl.multiple_of((1 - core) * half, half), half)
    for step in range(STEPS):
        out_ref[step, mine, :] = refs[step][0]
        out_ref[step, theirs, :] = swapped_ref[step]


def shards(tokens, base_weight, a_old, a_new, b_old, b_new, gains):
    rows, cols = tokens.shape
    tp = lax.axis_size("tp")
    t = lax.axis_index("tp")
    core = lax.rem(t, 2)
    half = rows // 2

    block = pl.pallas_call(
        block_kernel,
        out_shape=jax.ShapeDtypeStruct((2 * b_old.shape[1], cols), jnp.bfloat16),
        in_specs=[ANY] * 4,
        out_specs=VMEM,
        scratch_shapes=[
            pltpu.VMEM((2,) + a_new.shape, jnp.bfloat16),
            pltpu.VMEM((2,) + b_new.shape, jnp.bfloat16),
            pltpu.SemaphoreType.DMA((4,)),
        ],
        name="block",
    )(a_new, a_old, b_new, b_old)
    block, tokens = lax.optimization_barrier((block, tokens))
    block = lax.ppermute(block, ("fsdp", "tp"), SHIFTED)

    both = lax.all_gather(tokens, "tp", axis=0, axis_index_groups=PAIRS)
    both, base = lax.optimization_barrier((both, base_weight[0]))
    mate = lax.ppermute(base, "tp", SWAP)
    both = lax.dynamic_slice_in_dim(both, core * half, half, 1)
    stream = jnp.where(core == 0, both, both[::-1])
    x = spread(jnp.broadcast_to(stream.reshape(1, rows, cols), (CHIPS, rows, cols)))

    size = block.shape[0] // 2
    down, up = pl.pallas_call(
        split_kernel,
        out_shape=(
            jax.ShapeDtypeStruct((len(PLANES[0]), size, cols), jnp.bfloat16),
            jax.ShapeDtypeStruct((size, cols), jnp.bfloat16),
        ),
        in_specs=[VMEM],
        out_specs=(VMEM, VMEM),
        cost_estimate=pl.CostEstimate(flops=3 * 10**10, bytes_accessed=2**20, transcendentals=0),
        name="split",
        compiler_params=ROOM,
    )(block)
    down, up, x = lax.optimization_barrier((down, up, x))
    ups = [lax.ppermute(up, ("fsdp", "tp"), relay(part)) for part in range(2)]
    own = lax.all_to_all(down, ("fsdp", "tp"), 0, 0, axis_index_groups=PLANES)
    own, *ups = lax.optimization_barrier((own, *ups))
    other = lax.ppermute(own, "tp", SWAP)
    ups = lax.all_gather(jnp.stack(ups), "tp", axis=0, axis_index_groups=PAIRS)
    f = lax.axis_index("fsdp")
    place = jnp.stack([core, f // 16, f % 16])
    weights, merged = pl.pallas_call(
        merge_kernel,
        out_shape=(
            jax.ShapeDtypeStruct((tp, cols, 2 * cols), jnp.bfloat16),
            jax.ShapeDtypeStruct((tp * cols, cols), jnp.bfloat16),
        ),
        in_specs=[SMEM] + [VMEM] * 3 + [ANY] * 2,
        out_specs=(VMEM, ANY),
        scratch_shapes=[
            pltpu.VMEM((2, 2, cols // 2, cols), jnp.bfloat16),
            pltpu.VMEM((2, tp * cols, cols), jnp.bfloat16),
            pltpu.VMEM((tp * cols, cols), jnp.bfloat16),
            pltpu.SemaphoreType.DMA((2, CHIPS)),
            pltpu.SemaphoreType.DMA((CHIPS,)),
        ],
        name="merge",
        compiler_params=ROOM,
    )(place, own, other, ups, base_weight[0], mate)

    gain = gains[0].reshape(CHIPS, 2, 1, cols)
    gain = jnp.where(core == 0, gain, gain[:, ::-1]).reshape(tp, 1, cols)
    results, gives = [], []
    for step in range(STEPS):
        if step:
            x = spread(jnp.broadcast_to(stream.reshape(1, rows, cols), (CHIPS, rows, cols)))
        stream, give, weights = pl.pallas_call(
            step_kernel,
            out_shape=(
                jax.ShapeDtypeStruct((2, half, cols), jnp.bfloat16),
                jax.ShapeDtypeStruct((half, cols), jnp.bfloat16),
                jax.ShapeDtypeStruct(weights.shape, weights.dtype),
            ),
            in_specs=[VMEM] * 4,
            out_specs=(VMEM, VMEM, VMEM),
            input_output_aliases={1: 2},
            name="step",
            compiler_params=ROOM,
        )(x, weights, gain, stream)
        results.append(stream)
        gives.append(give)

    swapped = lax.ppermute(jnp.stack(gives), "tp", SWAP)
    ends = pl.pallas_call(
        finish_kernel,
        out_shape=jax.ShapeDtypeStruct((STEPS, rows, cols), jnp.bfloat16),
        in_specs=[SMEM] + [VMEM] * (STEPS + 1),
        out_specs=VMEM,
        name="finish",
        compiler_params=ROOM,
    )(core[None], swapped, *results)
    return ends, merged[None]


def solution(mesh):
    placed = (
        P("fsdp", "tp"),
        P(None, None, "tp"),
        P(None, "fsdp", None),
        P(None, "fsdp", None),
        P(None, "fsdp", None),
        P(None, "fsdp", None),
        P(),
    )
    return jax.shard_map(
        shards,
        mesh=mesh,
        in_specs=placed,
        out_specs=(P(None, "fsdp", "tp"), P(None, None, "tp")),
        check_vma=False,
    )
```

```python
import jax
import jax.numpy as jnp
from jax import lax
from jax.experimental import pallas as pl
from jax.experimental.pallas import tpu as pltpu
from jax.sharding import PartitionSpec as P

STEPS = 4
CHIPS = 8
GROUPS = [[2 * chip + core for chip in range(CHIPS)] for core in range(2)]
PAIRS = [[2 * chip, 2 * chip + 1] for chip in range(CHIPS)]
SWAP = [(i, i ^ 1) for i in range(2 * CHIPS)]
PLANES = [
    [(16 * (y % 2) + z) * 16 + 8 * (y // 2) + 2 * x + core for y in range(4) for x in range(4)]
    for z in range(16)
    for core in range(2)
]
SHIFTED = [
    ((16 * low + z) * 16 + t, (16 * low + (z + t // 2 + 8 * (t % 2)) % 16) * 16 + t)
    for low in range(2)
    for z in range(16)
    for t in range(16)
]


def relay(part):
    pairs = []
    for z in range(16):
        for low in range(2):
            for block in range(16):
                shift = (z - block) % 16
                source = (16 * low + z) * 16 + 2 * (shift % 8) + shift // 8
                target = 16 * ((block % 4 // 2) ^ part) + z
                pairs.append((source, target * 16 + 8 * low + 2 * (block // 4) + block % 2))
    return pairs


VMEM = pl.BlockSpec(memory_space=pltpu.VMEM)
SMEM = pl.BlockSpec(memory_space=pltpu.SMEM)
HBM = pl.BlockSpec(memory_space=pltpu.HBM)
WIDE = pltpu.CompilerParams(vmem_limit_bytes=32 * 1024 * 1024)
ROOM = pltpu.CompilerParams(vmem_limit_bytes=16 * 1024 * 1024)


def spread(blocks):
    return lax.all_to_all(blocks, "tp", 0, 0, axis_index_groups=GROUPS)


def block_kernel(a_new_ref, a_old_ref, b_new_ref, b_old_ref, out_ref, a_ref, b_ref, sems):
    copies = [
        pltpu.make_async_copy(source, target, sems.at[i])
        for i, (source, target) in enumerate(
            ((a_new_ref, a_ref.at[0]), (a_old_ref, a_ref.at[1]), (b_new_ref, b_ref.at[0]), (b_old_ref, b_ref.at[1]))
        )
    ]
    for copy in copies:
        copy.start()
    for copy in copies:
        copy.wait()
    half, cols = out_ref.shape[0] // 2, out_ref.shape[1]
    new = a_ref[0, 0].astype(jnp.float32)
    old = a_ref[1, 0].astype(jnp.float32)
    slices = []
    for i in range(new.shape[1] // cols):
        slices += [new[:, i * cols : (i + 1) * cols], old[:, i * cols : (i + 1) * cols]]
    out_ref[:half, :] = jnp.concatenate(slices, 0).astype(jnp.bfloat16)
    out_ref[half:, :] = jnp.concatenate([b_ref[0, 0], -b_ref[1, 0]], 1)


def split_kernel(block_ref, down_ref, up_ref):
    half = up_ref.shape[0]
    for chip in range(down_ref.shape[0]):
        down_ref[chip] = block_ref[:half, :]
    up_ref[...] = block_ref[half:, :]


def merge_kernel(
    place_ref, own_ref, other_ref, ups_ref, base_ref, mate_ref, weight_ref, merged_ref, up_ref, old_ref, new_ref, out_ref, in_sems, out_sems
):
    core, low, z = place_ref[0], place_ref[1], place_ref[2]
    cols = base_ref.shape[1]
    span = 2 * cols
    loads = []
    for pair in range(CHIPS):
        rows = slice(pair * span, (pair + 1) * span)
        loads.append(
            [
                pltpu.make_async_copy(ref.at[rows], old_ref.at[i, rows], in_sems.at[i, pair])
                for i, ref in enumerate((base_ref, mate_ref))
            ]
        )
        for load in loads[-1]:
            load.start()
    stores = []
    for left in range(2):
        for part in range(2):
            up_ref[lax.rem(part + low + core, 2), left] = ups_ref[left, part]
    goes = lax.broadcasted_iota(jnp.int32, (cols, cols), 0)
    comes = lax.broadcasted_iota(jnp.int32, (cols, cols), 1)
    chip = comes // 8 % 16
    shift = chip // 8 * 4 + chip % 4 + 8 * ((comes // 128 + core) % 2)
    block = chip // 4 % 2 * 16 + (z + 32 - shift) % 16
    place = comes // 4 % 2 * 128 + block * 4 + comes % 4
    order = jnp.where(place == goes, 1.0, 0.0).astype(jnp.bfloat16)
    up = jnp.dot(up_ref[...].reshape(2 * cols, cols), order, preferred_element_type=jnp.float32).astype(jnp.bfloat16)
    for pair in range(CHIPS):
        parts = [
            ref[:, 16 * pair : 16 * pair + 16, :].astype(jnp.float32).reshape(16, 2, 8, cols)
            for ref in (own_ref, other_ref)
        ]
        for load in loads[pair]:
            load.wait()
        for right in range(2):
            down = jnp.concatenate([part[:, right].reshape(128, cols) for part in parts], 0)
            down = down.T.astype(jnp.bfloat16)
            delta = lax.dot_general(down, up, (((1,), (1,)), ((), ())), preferred_element_type=jnp.float32)
            t = 2 * pair + right
            rows = slice(t * cols, (t + 1) * cols)
            mine = (old_ref[0, rows, :].astype(jnp.float32) + delta[:, :cols]).astype(jnp.bfloat16)
            theirs = (old_ref[1, rows, :].astype(jnp.float32) + delta[:, cols:]).astype(jnp.bfloat16)
            new_ref[rows, :] = mine
            which = 2 * pair + lax.rem(right + core, 2)
            out_ref[which, :, :cols] = mine
            out_ref[which, :, cols:] = theirs
        rows, both = slice(pair * span, (pair + 1) * span), slice(2 * pair, 2 * pair + 2)
        stores.append(pltpu.make_async_copy(new_ref.at[rows], merged_ref.at[rows], out_sems.at[0, pair]))
        stores.append(pltpu.make_async_copy(out_ref.at[both], weight_ref.at[both], out_sems.at[1, pair]))
        for store in stores[-2:]:
            store.start()
    for store in stores:
        store.wait()


def decode(x_ref, weight_ref, gain_ref, mine_ref, out_ref, give_ref, arrive):
    _, rows, cols = mine_ref.shape
    blocks = weight_ref.shape[0]
    part = lambda i: x_ref[i // 2, (i % 2) * rows : (i % 2 + 1) * rows, :].astype(jnp.float32)
    squares = part(0) * part(0)
    for i in range(1, blocks):
        squares += part(i) * part(i)
    mean = jnp.sum(squares, axis=1, keepdims=True) / (blocks * cols)
    scale = lax.rsqrt(mean + 1e-06)
    total = jnp.zeros((rows, 2 * cols), jnp.float32)
    for i in range(blocks):
        normed = (part(i) * scale * gain_ref[i]).astype(jnp.bfloat16)
        arrive(i)
        total += jnp.dot(normed, weight_ref[i], preferred_element_type=jnp.float32)
    for half in range(2):
        branch = total[:, half * cols : (half + 1) * cols]
        out_ref[half] = (mine_ref[half].astype(jnp.float32) + branch).astype(jnp.bfloat16)
    give_ref[...] = out_ref[1]


def first_kernel(x_ref, stored_ref, gain_ref, mine_ref, out_ref, give_ref, weight_ref, sems):
    loads = [
        pltpu.make_async_copy(stored_ref.at[2 * i : 2 * i + 2], weight_ref.at[2 * i : 2 * i + 2], sems.at[i])
        for i in range(CHIPS)
    ]
    for load in loads:
        load.start()

    def arrive(i):
        if i % 2 == 0:
            loads[i // 2].wait()

    decode(x_ref, weight_ref, gain_ref, mine_ref, out_ref, give_ref, arrive)


def step_kernel(x_ref, weight_ref, gain_ref, mine_ref, out_ref, give_ref, _):
    decode(x_ref, weight_ref, gain_ref, mine_ref, out_ref, give_ref, lambda i: None)


def finish_kernel(core_ref, swapped_ref, *refs):
    core = core_ref[0]
    out_ref = refs[-1]
    half = swapped_ref.shape[1]
    mine = pl.ds(pl.multiple_of(core * half, half), half)
    theirs = pl.ds(pl.multiple_of((1 - core) * half, half), half)
    for step in range(STEPS):
        out_ref[step, mine, :] = refs[step][0]
        out_ref[step, theirs, :] = swapped_ref[step]


def shards(tokens, base_weight, a_old, a_new, b_old, b_new, gains):
    rows, cols = tokens.shape
    tp = lax.axis_size("tp")
    t = lax.axis_index("tp")
    core = lax.rem(t, 2)
    half = rows // 2

    block = pl.pallas_call(
        block_kernel,
        out_shape=jax.ShapeDtypeStruct((2 * b_old.shape[1], cols), jnp.bfloat16),
        in_specs=[HBM] * 4,
        out_specs=VMEM,
        scratch_shapes=[
            pltpu.VMEM((2,) + a_new.shape, jnp.bfloat16),
            pltpu.VMEM((2,) + b_new.shape, jnp.bfloat16),
            pltpu.SemaphoreType.DMA((4,)),
        ],
        name="block",
    )(a_new, a_old, b_new, b_old)
    block, tokens = lax.optimization_barrier((block, tokens))
    block = lax.ppermute(block, ("fsdp", "tp"), SHIFTED)

    both = lax.all_gather(tokens, "tp", axis=0, axis_index_groups=PAIRS)
    both, base = lax.optimization_barrier((both, base_weight[0]))
    mate = lax.ppermute(base, "tp", SWAP)
    both = lax.dynamic_slice_in_dim(both, core * half, half, 1)
    stream = jnp.where(core == 0, both, both[::-1])

    size = block.shape[0] // 2
    down, up = pl.pallas_call(
        split_kernel,
        out_shape=(
            jax.ShapeDtypeStruct((len(PLANES[0]), size, cols), jnp.bfloat16),
            jax.ShapeDtypeStruct((size, cols), jnp.bfloat16),
        ),
        in_specs=[VMEM],
        out_specs=(VMEM, VMEM),
        name="split",
        compiler_params=ROOM,
    )(block)
    down, up, stream = lax.optimization_barrier((down, up, stream))
    ups = [lax.ppermute(up, ("fsdp", "tp"), relay(part)) for part in range(2)]
    own = lax.all_to_all(down, ("fsdp", "tp"), 0, 0, axis_index_groups=PLANES)
    own, stream, *ups = lax.optimization_barrier((own, stream, *ups))
    x = spread(jnp.broadcast_to(stream.reshape(1, rows, cols), (CHIPS, rows, cols)))
    other = lax.ppermute(own, "tp", SWAP)
    ups = lax.all_gather(jnp.stack(ups), "tp", axis=0, axis_index_groups=PAIRS)
    f = lax.axis_index("fsdp")
    place = jnp.stack([core, f // 16, f % 16])
    weights, merged = pl.pallas_call(
        merge_kernel,
        out_shape=(
            jax.ShapeDtypeStruct((tp, cols, 2 * cols), jnp.bfloat16),
            jax.ShapeDtypeStruct((tp * cols, cols), jnp.bfloat16),
        ),
        in_specs=[SMEM] + [VMEM] * 3 + [HBM] * 2,
        out_specs=(HBM, HBM),
        scratch_shapes=[
            pltpu.VMEM((2, 2, cols // 2, cols), jnp.bfloat16),
            pltpu.VMEM((2, tp * cols, cols), jnp.bfloat16),
            pltpu.VMEM((tp * cols, cols), jnp.bfloat16),
            pltpu.VMEM((tp, cols, 2 * cols), jnp.bfloat16),
            pltpu.SemaphoreType.DMA((2, CHIPS)),
            pltpu.SemaphoreType.DMA((2, CHIPS)),
        ],
        name="merge",
        compiler_params=WIDE,
    )(place, own, other, ups, base_weight[0], mate)

    gain = gains[0].reshape(CHIPS, 2, 1, cols)
    gain = jnp.where(core == 0, gain, gain[:, ::-1]).reshape(tp, 1, cols)
    results, gives = [], []
    for step in range(STEPS):
        if step:
            x = spread(jnp.broadcast_to(stream.reshape(1, rows, cols), (CHIPS, rows, cols)))
        stream, give, weights = pl.pallas_call(
            step_kernel if step else first_kernel,
            out_shape=(
                jax.ShapeDtypeStruct((2, half, cols), jnp.bfloat16),
                jax.ShapeDtypeStruct((half, cols), jnp.bfloat16),
                jax.ShapeDtypeStruct(weights.shape, weights.dtype),
            ),
            in_specs=[VMEM, VMEM if step else HBM, VMEM, VMEM],
            out_specs=(VMEM, VMEM, VMEM),
            scratch_shapes=[] if step else [pltpu.SemaphoreType.DMA((CHIPS,))],
            input_output_aliases={1: 2} if step else {},
            name="step" if step else "first",
            compiler_params=ROOM if step else pltpu.CompilerParams(vmem_limit_bytes=46 * 1024 * 1024),
        )(x, weights, gain, stream)
        results.append(stream)
        gives.append(give)

    swapped = lax.ppermute(jnp.stack(gives), "tp", SWAP)
    ends = pl.pallas_call(
        finish_kernel,
        out_shape=jax.ShapeDtypeStruct((STEPS, rows, cols), jnp.bfloat16),
        in_specs=[SMEM] + [VMEM] * (STEPS + 1),
        out_specs=VMEM,
        name="finish",
        compiler_params=ROOM,
    )(core[None], swapped, *results)
    return ends, merged[None]


def solution(mesh):
    placed = (
        P("fsdp", "tp"),
        P(None, None, "tp"),
        P(None, "fsdp", None),
        P(None, "fsdp", None),
        P(None, "fsdp", None),
        P(None, "fsdp", None),
        P(),
    )
    return jax.shard_map(
        shards,
        mesh=mesh,
        in_specs=placed,
        out_specs=(P(None, "fsdp", "tp"), P(None, None, "tp")),
        check_vma=False,
    )
```

```python
import jax
import jax.numpy as jnp
from jax import lax
from jax.experimental import pallas as pl
from jax.experimental.pallas import tpu as pltpu
from jax.sharding import PartitionSpec as P

STEPS = 4
CHIPS = 8
GROUPS = [[2 * chip + core for chip in range(CHIPS)] for core in range(2)]
PAIRS = [[2 * chip, 2 * chip + 1] for chip in range(CHIPS)]
SWAP = [(i, i ^ 1) for i in range(2 * CHIPS)]
PLANES = [
    [(16 * (y % 2) + z) * 16 + 8 * (y // 2) + 2 * x + core for y in range(4) for x in range(4)]
    for z in range(16)
    for core in range(2)
]
SHIFTED = [
    ((16 * low + z) * 16 + t, (16 * low + (z + t // 2 + 8 * (t % 2)) % 16) * 16 + t)
    for low in range(2)
    for z in range(16)
    for t in range(16)
]


def relay(part):
    pairs = []
    for z in range(16):
        for low in range(2):
            for block in range(16):
                shift = (z - block) % 16
                source = (16 * low + z) * 16 + 2 * (shift % 8) + shift // 8
                target = 16 * ((block % 4 // 2) ^ part) + z
                pairs.append((source, target * 16 + 8 * low + 2 * (block // 4) + block % 2))
    return pairs


VMEM = pl.BlockSpec(memory_space=pltpu.VMEM)
SMEM = pl.BlockSpec(memory_space=pltpu.SMEM)
HBM = pl.BlockSpec(memory_space=pltpu.HBM)
WIDE = pltpu.CompilerParams(vmem_limit_bytes=51 * 1024 * 1024)
ROOM = pltpu.CompilerParams(vmem_limit_bytes=16 * 1024 * 1024)


def spread(blocks):
    return lax.all_to_all(blocks, "tp", 0, 0, axis_index_groups=GROUPS)


def block_kernel(a_new_ref, a_old_ref, b_new_ref, b_old_ref, out_ref, a_ref, b_ref, sems):
    copies = [
        pltpu.make_async_copy(source, target, sems.at[i])
        for i, (source, target) in enumerate(
            ((a_new_ref, a_ref.at[0]), (a_old_ref, a_ref.at[1]), (b_new_ref, b_ref.at[0]), (b_old_ref, b_ref.at[1]))
        )
    ]
    for copy in copies:
        copy.start()
    for copy in copies:
        copy.wait()
    half, cols = out_ref.shape[0] // 2, out_ref.shape[1]
    new = a_ref[0, 0].astype(jnp.float32)
    old = a_ref[1, 0].astype(jnp.float32)
    slices = []
    for i in range(new.shape[1] // cols):
        slices += [new[:, i * cols : (i + 1) * cols], old[:, i * cols : (i + 1) * cols]]
    out_ref[:half, :] = jnp.concatenate(slices, 0).astype(jnp.bfloat16)
    out_ref[half:, :] = jnp.concatenate([b_ref[0, 0], -b_ref[1, 0]], 1)


def split_kernel(block_ref, down_ref, up_ref):
    half = up_ref.shape[0]
    for chip in range(down_ref.shape[0]):
        down_ref[chip] = block_ref[:half, :]
    up_ref[...] = block_ref[half:, :]


def merge_kernel(
    place_ref, own_ref, other_ref, ups_ref, base_ref, mate_ref, weight_ref, merged_ref, up_ref, old_ref, new_ref, out_ref, in_sems, out_sems
):
    core, low, z = place_ref[0], place_ref[1], place_ref[2]
    cols = base_ref.shape[1]
    span = 2 * cols
    loads = []
    for pair in range(CHIPS):
        rows = slice(pair * span, (pair + 1) * span)
        loads.append(
            [
                pltpu.make_async_copy(ref.at[rows], old_ref.at[i, rows], in_sems.at[i, pair])
                for i, ref in enumerate((base_ref, mate_ref))
            ]
        )
        for load in loads[-1]:
            load.start()
    stores = []
    for left in range(2):
        for part in range(2):
            up_ref[lax.rem(part + low + core, 2), left] = ups_ref[left, part]
    goes = lax.broadcasted_iota(jnp.int32, (cols, cols), 0)
    comes = lax.broadcasted_iota(jnp.int32, (cols, cols), 1)
    chip = comes // 8 % 16
    shift = chip // 8 * 4 + chip % 4 + 8 * ((comes // 128 + core) % 2)
    block = chip // 4 % 2 * 16 + (z + 32 - shift) % 16
    place = comes // 4 % 2 * 128 + block * 4 + comes % 4
    order = jnp.where(place == goes, 1.0, 0.0).astype(jnp.bfloat16)
    up = jnp.dot(up_ref[...].reshape(2 * cols, cols), order, preferred_element_type=jnp.float32).astype(jnp.bfloat16)
    for pair in range(CHIPS):
        parts = [
            ref[:, 16 * pair : 16 * pair + 16, :].astype(jnp.float32).reshape(16, 2, 8, cols)
            for ref in (own_ref, other_ref)
        ]
        for load in loads[pair]:
            load.wait()
        for right in range(2):
            down = jnp.concatenate([part[:, right].reshape(128, cols) for part in parts], 0)
            down = down.astype(jnp.bfloat16).T
            delta = lax.dot_general(down, up, (((1,), (1,)), ((), ())), preferred_element_type=jnp.float32)
            t = 2 * pair + right
            rows = slice(t * cols, (t + 1) * cols)
            mine = (old_ref[0, rows, :].astype(jnp.float32) + delta[:, :cols]).astype(jnp.bfloat16)
            theirs = (old_ref[1, rows, :].astype(jnp.float32) + delta[:, cols:]).astype(jnp.bfloat16)
            new_ref[rows, :] = mine
            which = 2 * pair + lax.rem(right + core, 2)
            out_ref[which, :, :cols] = mine
            out_ref[which, :, cols:] = theirs
        rows, both = slice(pair * span, (pair + 1) * span), slice(2 * pair, 2 * pair + 2)
        stores.append(pltpu.make_async_copy(new_ref.at[rows], merged_ref.at[rows], out_sems.at[0, pair]))
        stores.append(pltpu.make_async_copy(out_ref.at[both], weight_ref.at[both], out_sems.at[1, pair]))
        for store in stores[-2:]:
            store.start()
    for store in stores:
        store.wait()


def decode(x_ref, weight_ref, gain_ref, mine_ref, out_ref, give_ref, arrive):
    _, rows, cols = mine_ref.shape
    blocks = weight_ref.shape[0]
    part = lambda i: x_ref[i // 2, (i % 2) * rows : (i % 2 + 1) * rows, :].astype(jnp.float32)
    squares = part(0) * part(0)
    for i in range(1, blocks):
        squares += part(i) * part(i)
    mean = jnp.sum(squares, axis=1, keepdims=True) / (blocks * cols)
    scale = lax.rsqrt(mean + 1e-06)
    total = jnp.zeros((rows, 2 * cols), jnp.float32)
    for i in range(blocks):
        normed = (part(i) * scale * gain_ref[i]).astype(jnp.bfloat16)
        arrive(i)
        total += jnp.dot(normed, weight_ref[i], preferred_element_type=jnp.float32)
    for half in range(2):
        branch = total[:, half * cols : (half + 1) * cols]
        out_ref[half] = (mine_ref[half].astype(jnp.float32) + branch).astype(jnp.bfloat16)
    give_ref[...] = out_ref[1]


def first_kernel(x_ref, stored_ref, gain_ref, mine_ref, out_ref, give_ref, weight_ref, sems):
    loads = [
        pltpu.make_async_copy(stored_ref.at[2 * i : 2 * i + 2], weight_ref.at[2 * i : 2 * i + 2], sems.at[i])
        for i in range(CHIPS)
    ]
    for load in loads:
        load.start()

    def arrive(i):
        if i % 2 == 0:
            loads[i // 2].wait()

    decode(x_ref, weight_ref, gain_ref, mine_ref, out_ref, give_ref, arrive)


def step_kernel(x_ref, weight_ref, gain_ref, mine_ref, out_ref, give_ref, _):
    decode(x_ref, weight_ref, gain_ref, mine_ref, out_ref, give_ref, lambda i: None)


def finish_kernel(core_ref, swapped_ref, *refs):
    core = core_ref[0]
    out_ref = refs[-1]
    half = swapped_ref.shape[1]
    mine = pl.ds(pl.multiple_of(core * half, half), half)
    theirs = pl.ds(pl.multiple_of((1 - core) * half, half), half)
    for step in range(STEPS):
        out_ref[step, mine, :] = refs[step][0]
        out_ref[step, theirs, :] = swapped_ref[step]


def shards(tokens, base_weight, a_old, a_new, b_old, b_new, gains):
    rows, cols = tokens.shape
    tp = lax.axis_size("tp")
    t = lax.axis_index("tp")
    core = lax.rem(t, 2)
    half = rows // 2

    block = pl.pallas_call(
        block_kernel,
        out_shape=jax.ShapeDtypeStruct((2 * b_old.shape[1], cols), jnp.bfloat16),
        in_specs=[HBM] * 4,
        out_specs=VMEM,
        scratch_shapes=[
            pltpu.VMEM((2,) + a_new.shape, jnp.bfloat16),
            pltpu.VMEM((2,) + b_new.shape, jnp.bfloat16),
            pltpu.SemaphoreType.DMA((4,)),
        ],
        name="block",
    )(a_new, a_old, b_new, b_old)
    block, tokens = lax.optimization_barrier((block, tokens))
    block = lax.ppermute(block, ("fsdp", "tp"), SHIFTED)

    both = lax.all_gather(tokens, "tp", axis=0, axis_index_groups=PAIRS)
    both, base = lax.optimization_barrier((both, base_weight[0]))
    mate = lax.ppermute(base, "tp", SWAP)
    both = lax.dynamic_slice_in_dim(both, core * half, half, 1)
    stream = jnp.where(core == 0, both, both[::-1])

    size = block.shape[0] // 2
    down, up = pl.pallas_call(
        split_kernel,
        out_shape=(
            jax.ShapeDtypeStruct((len(PLANES[0]), size, cols), jnp.bfloat16),
            jax.ShapeDtypeStruct((size, cols), jnp.bfloat16),
        ),
        in_specs=[VMEM],
        out_specs=(VMEM, VMEM),
        name="split",
        compiler_params=ROOM,
    )(block)
    down, up, stream = lax.optimization_barrier((down, up, stream))
    ups = [lax.ppermute(up, ("fsdp", "tp"), relay(part)) for part in range(2)]
    own = lax.all_to_all(down, ("fsdp", "tp"), 0, 0, axis_index_groups=PLANES)
    own, stream, *ups = lax.optimization_barrier((own, stream, *ups))
    x = spread(jnp.broadcast_to(stream.reshape(1, rows, cols), (CHIPS, rows, cols)))
    other = lax.ppermute(own, "tp", SWAP)
    ups = lax.all_gather(jnp.stack(ups), "tp", axis=0, axis_index_groups=PAIRS)
    f = lax.axis_index("fsdp")
    place = jnp.stack([core, f // 16, f % 16])
    weights, merged = pl.pallas_call(
        merge_kernel,
        out_shape=(
            jax.ShapeDtypeStruct((tp, cols, 2 * cols), jnp.bfloat16),
            jax.ShapeDtypeStruct((tp * cols, cols), jnp.bfloat16),
        ),
        in_specs=[SMEM] + [VMEM] * 3 + [HBM] * 2,
        out_specs=(HBM, HBM),
        scratch_shapes=[
            pltpu.VMEM((2, 2, cols // 2, cols), jnp.bfloat16),
            pltpu.VMEM((2, tp * cols, cols), jnp.bfloat16),
            pltpu.VMEM((tp * cols, cols), jnp.bfloat16),
            pltpu.VMEM((tp, cols, 2 * cols), jnp.bfloat16),
            pltpu.SemaphoreType.DMA((2, CHIPS)),
            pltpu.SemaphoreType.DMA((2, CHIPS)),
        ],
        name="merge",
        compiler_params=WIDE,
    )(place, own, other, ups, base_weight[0], mate)

    gain = gains[0].reshape(CHIPS, 2, 1, cols)
    gain = jnp.where(core == 0, gain, gain[:, ::-1]).reshape(tp, 1, cols)
    results, gives = [], []
    for step in range(STEPS):
        if step:
            x = spread(jnp.broadcast_to(stream.reshape(1, rows, cols), (CHIPS, rows, cols)))
        stream, give, weights = pl.pallas_call(
            step_kernel if step else first_kernel,
            out_shape=(
                jax.ShapeDtypeStruct((2, half, cols), jnp.bfloat16),
                jax.ShapeDtypeStruct((half, cols), jnp.bfloat16),
                jax.ShapeDtypeStruct(weights.shape, weights.dtype),
            ),
            in_specs=[VMEM, VMEM if step else HBM, VMEM, VMEM],
            out_specs=(VMEM, VMEM, VMEM),
            scratch_shapes=[] if step else [pltpu.SemaphoreType.DMA((CHIPS,))],
            input_output_aliases={1: 2} if step else {},
            name="step" if step else "first",
            compiler_params=ROOM if step else pltpu.CompilerParams(vmem_limit_bytes=46 * 1024 * 1024),
        )(x, weights, gain, stream)
        results.append(stream)
        gives.append(give)

    swapped = lax.ppermute(jnp.stack(gives), "tp", SWAP)
    ends = pl.pallas_call(
        finish_kernel,
        out_shape=jax.ShapeDtypeStruct((STEPS, rows, cols), jnp.bfloat16),
        in_specs=[SMEM] + [VMEM] * (STEPS + 1),
        out_specs=VMEM,
        name="finish",
        compiler_params=ROOM,
    )(core[None], swapped, *results)
    return ends, merged[None]


def solution(mesh):
    placed = (
        P("fsdp", "tp"),
        P(None, None, "tp"),
        P(None, "fsdp", None),
        P(None, "fsdp", None),
        P(None, "fsdp", None),
        P(None, "fsdp", None),
        P(),
    )
    return jax.shard_map(
        shards,
        mesh=mesh,
        in_specs=placed,
        out_specs=(P(None, "fsdp", "tp"), P(None, None, "tp")),
        check_vma=False,
    )
```

```python
import jax
import jax.numpy as jnp
from jax import lax
from jax.experimental import pallas as pl
from jax.experimental.pallas import tpu as pltpu
from jax.sharding import PartitionSpec as P

STEPS = 4
CHIPS = 8
GROUPS = [[2 * chip + core for chip in range(CHIPS)] for core in range(2)]
PAIRS = [[2 * chip, 2 * chip + 1] for chip in range(CHIPS)]
SWAP = [(i, i ^ 1) for i in range(2 * CHIPS)]
PLANES = [
    [(16 * (y % 2) + z) * 16 + 8 * (y // 2) + 2 * x + core for y in range(4) for x in range(4)]
    for z in range(16)
    for core in range(2)
]
DOWN_SHIFTS = [(t // 2 + 8 * (t % 2)) % 16 for t in range(16)]
UP_SHIFTS = [(8 * (t % 2) - t // 2) % 16 for t in range(16)]


def shifted(shifts):
    return [
        ((16 * low + z) * 16 + t, (16 * low + (z + shifts[t]) % 16) * 16 + t)
        for low in range(2)
        for z in range(16)
        for t in range(16)
    ]


def relay(part):
    pairs = []
    for z in range(16):
        for low in range(2):
            for block in range(16):
                source = (16 * low + z) * 16 + UP_SHIFTS.index((z - block) % 16)
                target = 16 * ((block % 4 // 2) ^ part) + z
                pairs.append((source, target * 16 + 8 * low + 2 * (block // 4) + block % 2))
    return pairs


VMEM = pl.BlockSpec(memory_space=pltpu.VMEM)
SMEM = pl.BlockSpec(memory_space=pltpu.SMEM)
HBM = pl.BlockSpec(memory_space=pltpu.HBM)
WIDE = pltpu.CompilerParams(vmem_limit_bytes=51 * 1024 * 1024)
ROOM = pltpu.CompilerParams(vmem_limit_bytes=16 * 1024 * 1024)


def spread(blocks):
    return lax.all_to_all(blocks, "tp", 0, 0, axis_index_groups=GROUPS)


def block_kernel(a_new_ref, a_old_ref, b_new_ref, b_old_ref, down_ref, up_ref, a_ref, b_ref, sems):
    copies = [
        pltpu.make_async_copy(source, target, sems.at[i])
        for i, (source, target) in enumerate(
            ((a_new_ref, a_ref.at[0]), (a_old_ref, a_ref.at[1]), (b_new_ref, b_ref.at[0]), (b_old_ref, b_ref.at[1]))
        )
    ]
    for copy in copies:
        copy.start()
    for copy in copies:
        copy.wait()
    cols = down_ref.shape[1]
    new = a_ref[0, 0].astype(jnp.float32)
    old = a_ref[1, 0].astype(jnp.float32)
    slices = []
    for i in range(new.shape[1] // cols):
        slices += [new[:, i * cols : (i + 1) * cols], old[:, i * cols : (i + 1) * cols]]
    down_ref[...] = jnp.concatenate(slices, 0).astype(jnp.bfloat16)
    up_ref[...] = jnp.concatenate([b_ref[0, 0], -b_ref[1, 0]], 1)


def merge_kernel(
    place_ref, own_ref, other_ref, ups_ref, base_ref, mate_ref, weight_ref, merged_ref, up_ref, old_ref, new_ref, out_ref, in_sems, out_sems
):
    core, low, z = place_ref[0], place_ref[1], place_ref[2]
    cols = base_ref.shape[1]
    span = 2 * cols
    loads = []
    for pair in range(CHIPS):
        rows = slice(pair * span, (pair + 1) * span)
        loads.append(
            [
                pltpu.make_async_copy(ref.at[rows], old_ref.at[i, rows], in_sems.at[i, pair])
                for i, ref in enumerate((base_ref, mate_ref))
            ]
        )
        for load in loads[-1]:
            load.start()
    stores = []
    for left in range(2):
        for part in range(2):
            up_ref[lax.rem(part + low + core, 2), left] = ups_ref[left, part]
    goes = lax.broadcasted_iota(jnp.int32, (cols, cols), 0)
    comes = lax.broadcasted_iota(jnp.int32, (cols, cols), 1)
    chip = comes // 8 % 16
    shift = chip // 8 * 4 + chip % 4 + 8 * ((comes // 128 + core) % 2)
    block = chip // 4 % 2 * 16 + (z + 32 - shift) % 16
    place = comes // 4 % 2 * 128 + block * 4 + comes % 4
    order = jnp.where(place == goes, 1.0, 0.0).astype(jnp.bfloat16)
    up = jnp.dot(up_ref[...].reshape(2 * cols, cols), order, preferred_element_type=jnp.float32).astype(jnp.bfloat16)
    for pair in range(CHIPS):
        parts = [
            ref[:, 16 * pair : 16 * pair + 16, :].astype(jnp.float32).reshape(16, 2, 8, cols)
            for ref in (own_ref, other_ref)
        ]
        for load in loads[pair]:
            load.wait()
        for right in range(2):
            down = jnp.concatenate([part[:, right].reshape(128, cols) for part in parts], 0)
            down = down.astype(jnp.bfloat16).T
            delta = lax.dot_general(down, up, (((1,), (1,)), ((), ())), preferred_element_type=jnp.float32)
            t = 2 * pair + right
            rows = slice(t * cols, (t + 1) * cols)
            mine = (old_ref[0, rows, :].astype(jnp.float32) + delta[:, :cols]).astype(jnp.bfloat16)
            theirs = (old_ref[1, rows, :].astype(jnp.float32) + delta[:, cols:]).astype(jnp.bfloat16)
            new_ref[rows, :] = mine
            which = 2 * pair + lax.rem(right + core, 2)
            out_ref[which, :, :cols] = mine
            out_ref[which, :, cols:] = theirs
        rows, both = slice(pair * span, (pair + 1) * span), slice(2 * pair, 2 * pair + 2)
        stores.append(pltpu.make_async_copy(new_ref.at[rows], merged_ref.at[rows], out_sems.at[0, pair]))
        stores.append(pltpu.make_async_copy(out_ref.at[both], weight_ref.at[both], out_sems.at[1, pair]))
        for store in stores[-2:]:
            store.start()
    for store in stores:
        store.wait()


def decode(x_ref, weight_ref, gain_ref, mine_ref, out_ref, give_ref, arrive):
    _, rows, cols = mine_ref.shape
    blocks = weight_ref.shape[0]
    part = lambda i: x_ref[i // 2, (i % 2) * rows : (i % 2 + 1) * rows, :].astype(jnp.float32)
    squares = part(0) * part(0)
    for i in range(1, blocks):
        squares += part(i) * part(i)
    mean = jnp.sum(squares, axis=1, keepdims=True) / (blocks * cols)
    scale = lax.rsqrt(mean + 1e-06)
    total = jnp.zeros((rows, 2 * cols), jnp.float32)
    for i in range(blocks):
        normed = (part(i) * scale * gain_ref[i]).astype(jnp.bfloat16)
        arrive(i)
        total += jnp.dot(normed, weight_ref[i], preferred_element_type=jnp.float32)
    for half in range(2):
        branch = total[:, half * cols : (half + 1) * cols]
        out_ref[half] = (mine_ref[half].astype(jnp.float32) + branch).astype(jnp.bfloat16)
    give_ref[...] = out_ref[1]


def first_kernel(x_ref, stored_ref, gain_ref, mine_ref, out_ref, give_ref, weight_ref, sems):
    loads = [
        pltpu.make_async_copy(stored_ref.at[2 * i : 2 * i + 2], weight_ref.at[2 * i : 2 * i + 2], sems.at[i])
        for i in range(CHIPS)
    ]
    for load in loads:
        load.start()

    def arrive(i):
        if i % 2 == 0:
            loads[i // 2].wait()

    decode(x_ref, weight_ref, gain_ref, mine_ref, out_ref, give_ref, arrive)


def step_kernel(x_ref, weight_ref, gain_ref, mine_ref, out_ref, give_ref, _):
    decode(x_ref, weight_ref, gain_ref, mine_ref, out_ref, give_ref, lambda i: None)


def finish_kernel(core_ref, swapped_ref, *refs):
    core = core_ref[0]
    out_ref = refs[-1]
    half = swapped_ref.shape[1]
    mine = pl.ds(pl.multiple_of(core * half, half), half)
    theirs = pl.ds(pl.multiple_of((1 - core) * half, half), half)
    for step in range(STEPS):
        out_ref[step, mine, :] = refs[step][0]
        out_ref[step, theirs, :] = swapped_ref[step]


def shards(tokens, base_weight, a_old, a_new, b_old, b_new, gains):
    rows, cols = tokens.shape
    tp = lax.axis_size("tp")
    t = lax.axis_index("tp")
    core = lax.rem(t, 2)
    half = rows // 2

    size = b_old.shape[1]
    down, up = pl.pallas_call(
        block_kernel,
        out_shape=(jax.ShapeDtypeStruct((size, cols), jnp.bfloat16),) * 2,
        in_specs=[HBM] * 4,
        out_specs=(VMEM, VMEM),
        scratch_shapes=[
            pltpu.VMEM((2,) + a_new.shape, jnp.bfloat16),
            pltpu.VMEM((2,) + b_new.shape, jnp.bfloat16),
            pltpu.SemaphoreType.DMA((4,)),
        ],
        name="block",
    )(a_new, a_old, b_new, b_old)
    down, up, tokens = lax.optimization_barrier((down, up, tokens))
    down = lax.ppermute(down, ("fsdp", "tp"), shifted(DOWN_SHIFTS))
    up = lax.ppermute(up, ("fsdp", "tp"), shifted(UP_SHIFTS))

    both = lax.all_gather(tokens, "tp", axis=0, axis_index_groups=PAIRS)
    both, base = lax.optimization_barrier((both, base_weight[0]))
    mate = lax.ppermute(base, "tp", SWAP)
    both = lax.dynamic_slice_in_dim(both, core * half, half, 1)
    stream = jnp.where(core == 0, both, both[::-1])

    down, up, stream = lax.optimization_barrier((down, up, stream))
    down = jnp.broadcast_to(down[None], (len(PLANES[0]), size, cols))
    ups = [lax.ppermute(up, ("fsdp", "tp"), relay(part)) for part in range(2)]
    own = lax.all_to_all(down, ("fsdp", "tp"), 0, 0, axis_index_groups=PLANES)
    own, stream, *ups = lax.optimization_barrier((own, stream, *ups))
    x = spread(jnp.broadcast_to(stream.reshape(1, rows, cols), (CHIPS, rows, cols)))
    other = lax.ppermute(own, "tp", SWAP)
    ups = lax.all_gather(jnp.stack(ups), "tp", axis=0, axis_index_groups=PAIRS)
    f = lax.axis_index("fsdp")
    place = jnp.stack([core, f // 16, f % 16])
    weights, merged = pl.pallas_call(
        merge_kernel,
        out_shape=(
            jax.ShapeDtypeStruct((tp, cols, 2 * cols), jnp.bfloat16),
            jax.ShapeDtypeStruct((tp * cols, cols), jnp.bfloat16),
        ),
        in_specs=[SMEM] + [VMEM] * 3 + [HBM] * 2,
        out_specs=(HBM, HBM),
        scratch_shapes=[
            pltpu.VMEM((2, 2, cols // 2, cols), jnp.bfloat16),
            pltpu.VMEM((2, tp * cols, cols), jnp.bfloat16),
            pltpu.VMEM((tp * cols, cols), jnp.bfloat16),
            pltpu.VMEM((tp, cols, 2 * cols), jnp.bfloat16),
            pltpu.SemaphoreType.DMA((2, CHIPS)),
            pltpu.SemaphoreType.DMA((2, CHIPS)),
        ],
        name="merge",
        compiler_params=WIDE,
    )(place, own, other, ups, base_weight[0], mate)

    gain = gains[0].reshape(CHIPS, 2, 1, cols)
    gain = jnp.where(core == 0, gain, gain[:, ::-1]).reshape(tp, 1, cols)
    results, gives = [], []
    for step in range(STEPS):
        if step:
            x = spread(jnp.broadcast_to(stream.reshape(1, rows, cols), (CHIPS, rows, cols)))
        stream, give, weights = pl.pallas_call(
            step_kernel if step else first_kernel,
            out_shape=(
                jax.ShapeDtypeStruct((2, half, cols), jnp.bfloat16),
                jax.ShapeDtypeStruct((half, cols), jnp.bfloat16),
                jax.ShapeDtypeStruct(weights.shape, weights.dtype),
            ),
            in_specs=[VMEM, VMEM if step else HBM, VMEM, VMEM],
            out_specs=(VMEM, VMEM, VMEM),
            scratch_shapes=[] if step else [pltpu.SemaphoreType.DMA((CHIPS,))],
            input_output_aliases={1: 2} if step else {},
            name="step" if step else "first",
            compiler_params=ROOM if step else pltpu.CompilerParams(vmem_limit_bytes=46 * 1024 * 1024),
        )(x, weights, gain, stream)
        results.append(stream)
        gives.append(give)

    swapped = lax.ppermute(jnp.stack(gives), "tp", SWAP)
    ends = pl.pallas_call(
        finish_kernel,
        out_shape=jax.ShapeDtypeStruct((STEPS, rows, cols), jnp.bfloat16),
        in_specs=[SMEM] + [VMEM] * (STEPS + 1),
        out_specs=VMEM,
        name="finish",
        compiler_params=ROOM,
    )(core[None], swapped, *results)
    return ends, merged[None]


def solution(mesh):
    placed = (
        P("fsdp", "tp"),
        P(None, None, "tp"),
        P(None, "fsdp", None),
        P(None, "fsdp", None),
        P(None, "fsdp", None),
        P(None, "fsdp", None),
        P(),
    )
    return jax.shard_map(
        shards,
        mesh=mesh,
        in_specs=placed,
        out_specs=(P(None, "fsdp", "tp"), P(None, None, "tp")),
        check_vma=False,
    )
```

```python
import jax
import jax.numpy as jnp
from jax import lax
from jax.experimental import pallas as pl
from jax.experimental.pallas import tpu as pltpu
from jax.sharding import PartitionSpec as P

STEPS = 4
CHIPS = 8
GROUPS = [[2 * chip + core for chip in range(CHIPS)] for core in range(2)]
PAIRS = [[2 * chip, 2 * chip + 1] for chip in range(CHIPS)]
SWAP = [(i, i ^ 1) for i in range(2 * CHIPS)]
PLANES = [
    [(16 * (y % 2) + z) * 16 + 8 * (y // 2) + 2 * x + core for y in range(4) for x in range(4)]
    for z in range(16)
    for core in range(2)
]
SHIFTED = [
    ((16 * low + z) * 16 + t, (16 * low + (z + t // 2 + 8 * (t % 2)) % 16) * 16 + t)
    for low in range(2)
    for z in range(16)
    for t in range(16)
]


def relay(part):
    pairs = []
    for z in range(16):
        for low in range(2):
            for block in range(16):
                shift = (z - block) % 16
                source = (16 * low + z) * 16 + 2 * (shift % 8) + shift // 8
                target = 16 * ((block % 4 // 2) ^ part) + z
                pairs.append((source, target * 16 + 8 * low + 2 * (block // 4) + block % 2))
    return pairs


VMEM = pl.BlockSpec(memory_space=pltpu.VMEM)
SMEM = pl.BlockSpec(memory_space=pltpu.SMEM)
HBM = pl.BlockSpec(memory_space=pltpu.HBM)
WIDE = pltpu.CompilerParams(vmem_limit_bytes=51 * 1024 * 1024)
ROOM = pltpu.CompilerParams(vmem_limit_bytes=16 * 1024 * 1024)


def spread(blocks):
    return lax.all_to_all(blocks, "tp", 0, 0, axis_index_groups=GROUPS)


def block_kernel(a_new_ref, a_old_ref, b_new_ref, b_old_ref, out_ref, a_ref, b_ref, sems):
    copies = [
        pltpu.make_async_copy(source, target, sems.at[i])
        for i, (source, target) in enumerate(
            ((a_new_ref, a_ref.at[0]), (a_old_ref, a_ref.at[1]), (b_new_ref, b_ref.at[0]), (b_old_ref, b_ref.at[1]))
        )
    ]
    for copy in copies:
        copy.start()
    for copy in copies:
        copy.wait()
    half, cols = out_ref.shape[0] // 2, out_ref.shape[1]
    new = a_ref[0, 0].astype(jnp.float32)
    old = a_ref[1, 0].astype(jnp.float32)
    slices = []
    for i in range(new.shape[1] // cols):
        slices += [new[:, i * cols : (i + 1) * cols], old[:, i * cols : (i + 1) * cols]]
    out_ref[:half, :] = jnp.concatenate(slices, 0).astype(jnp.bfloat16)
    out_ref[half:, :] = jnp.concatenate([b_ref[0, 0], -b_ref[1, 0]], 1)


def split_kernel(block_ref, down_ref, up_ref):
    half = up_ref.shape[0]
    for chip in range(down_ref.shape[0]):
        down_ref[chip] = block_ref[:half, :]
    up_ref[...] = block_ref[half:, :]


def merge_kernel(
    place_ref, own_ref, other_ref, ups_ref, base_ref, mate_ref, weight_ref, merged_ref, up_ref, old_ref, new_ref, out_ref, turned_ref, in_sems, out_sems
):
    core, low, z = place_ref[0], place_ref[1], place_ref[2]
    cols = base_ref.shape[1]
    loads = [
        pltpu.make_async_copy(ref, old_ref.at[i], in_sems.at[i]) for i, ref in enumerate((base_ref, mate_ref))
    ]
    for load in loads:
        load.start()
    stores = []
    for left in range(2):
        for part in range(2):
            up_ref[lax.rem(part + low + core, 2), left] = ups_ref[left, part]
    goes = lax.broadcasted_iota(jnp.int32, (cols, cols), 0)
    comes = lax.broadcasted_iota(jnp.int32, (cols, cols), 1)
    chip = comes // 8 % 16
    shift = chip // 8 * 4 + chip % 4 + 8 * ((comes // 128 + core) % 2)
    block = chip // 4 % 2 * 16 + (z + 32 - shift) % 16
    place = comes // 4 % 2 * 128 + block * 4 + comes % 4
    order = jnp.where(place == goes, 1.0, 0.0).astype(jnp.bfloat16)
    up = jnp.dot(up_ref[...].reshape(2 * cols, cols), order, preferred_element_type=jnp.float32).astype(jnp.bfloat16)
    for pair in range(CHIPS):
        parts = [
            ref[:, 16 * pair : 16 * pair + 16, :].astype(jnp.float32).reshape(16, 2, 8, cols)
            for ref in (own_ref, other_ref)
        ]
        for right in range(2):
            down = jnp.concatenate([part[:, right].reshape(128, cols) for part in parts], 0)
            turned_ref[2 * pair + right] = down.astype(jnp.bfloat16).T
    for load in loads:
        load.wait()
    for quarter in range(4):
        for t in range(4 * quarter, 4 * quarter + 4):
            delta = lax.dot_general(turned_ref[t], up, (((1,), (1,)), ((), ())), preferred_element_type=jnp.float32)
            rows = slice(t * cols, (t + 1) * cols)
            mine = (old_ref[0, rows, :].astype(jnp.float32) + delta[:, :cols]).astype(jnp.bfloat16)
            theirs = (old_ref[1, rows, :].astype(jnp.float32) + delta[:, cols:]).astype(jnp.bfloat16)
            new_ref[rows, :] = mine
            which = t // 2 * 2 + lax.rem(t + core, 2)
            out_ref[which, :, :cols] = mine
            out_ref[which, :, cols:] = theirs
        rows, blocks = slice(4 * quarter * cols, (4 * quarter + 4) * cols), slice(4 * quarter, 4 * quarter + 4)
        stores.append(pltpu.make_async_copy(new_ref.at[rows], merged_ref.at[rows], out_sems.at[0, quarter]))
        stores.append(pltpu.make_async_copy(out_ref.at[blocks], weight_ref.at[blocks], out_sems.at[1, quarter]))
        for store in stores[-2:]:
            store.start()
    for store in stores:
        store.wait()


def decode(x_ref, weight_ref, gain_ref, mine_ref, out_ref, give_ref, arrive):
    _, rows, cols = mine_ref.shape
    blocks = weight_ref.shape[0]
    part = lambda i: x_ref[i // 2, (i % 2) * rows : (i % 2 + 1) * rows, :].astype(jnp.float32)
    squares = part(0) * part(0)
    for i in range(1, blocks):
        squares += part(i) * part(i)
    mean = jnp.sum(squares, axis=1, keepdims=True) / (blocks * cols)
    scale = lax.rsqrt(mean + 1e-06)
    total = jnp.zeros((rows, 2 * cols), jnp.float32)
    for i in range(blocks):
        normed = (part(i) * scale * gain_ref[i]).astype(jnp.bfloat16)
        arrive(i)
        total += jnp.dot(normed, weight_ref[i], preferred_element_type=jnp.float32)
    for half in range(2):
        branch = total[:, half * cols : (half + 1) * cols]
        out_ref[half] = (mine_ref[half].astype(jnp.float32) + branch).astype(jnp.bfloat16)
    give_ref[...] = out_ref[1]


def first_kernel(x_ref, stored_ref, gain_ref, mine_ref, out_ref, give_ref, weight_ref, sems):
    loads = [
        pltpu.make_async_copy(stored_ref.at[2 * i : 2 * i + 2], weight_ref.at[2 * i : 2 * i + 2], sems.at[i])
        for i in range(CHIPS)
    ]
    for load in loads:
        load.start()

    def arrive(i):
        if i % 2 == 0:
            loads[i // 2].wait()

    decode(x_ref, weight_ref, gain_ref, mine_ref, out_ref, give_ref, arrive)


def step_kernel(x_ref, weight_ref, gain_ref, mine_ref, out_ref, give_ref, _):
    decode(x_ref, weight_ref, gain_ref, mine_ref, out_ref, give_ref, lambda i: None)


def finish_kernel(core_ref, swapped_ref, *refs):
    core = core_ref[0]
    out_ref = refs[-1]
    half = swapped_ref.shape[1]
    mine = pl.ds(pl.multiple_of(core * half, half), half)
    theirs = pl.ds(pl.multiple_of((1 - core) * half, half), half)
    for step in range(STEPS):
        out_ref[step, mine, :] = refs[step][0]
        out_ref[step, theirs, :] = swapped_ref[step]


def shards(tokens, base_weight, a_old, a_new, b_old, b_new, gains):
    rows, cols = tokens.shape
    tp = lax.axis_size("tp")
    t = lax.axis_index("tp")
    core = lax.rem(t, 2)
    half = rows // 2

    block = pl.pallas_call(
        block_kernel,
        out_shape=jax.ShapeDtypeStruct((2 * b_old.shape[1], cols), jnp.bfloat16),
        in_specs=[HBM] * 4,
        out_specs=VMEM,
        scratch_shapes=[
            pltpu.VMEM((2,) + a_new.shape, jnp.bfloat16),
            pltpu.VMEM((2,) + b_new.shape, jnp.bfloat16),
            pltpu.SemaphoreType.DMA((4,)),
        ],
        name="block",
    )(a_new, a_old, b_new, b_old)
    block, tokens = lax.optimization_barrier((block, tokens))
    block = lax.ppermute(block, ("fsdp", "tp"), SHIFTED)

    both = lax.all_gather(tokens, "tp", axis=0, axis_index_groups=PAIRS)
    both = lax.dynamic_slice_in_dim(both, core * half, half, 1)
    stream = jnp.where(core == 0, both, both[::-1])
    copies = jnp.broadcast_to(stream.reshape(1, rows, cols), (CHIPS, rows, cols))
    copies, base = lax.optimization_barrier((copies, base_weight[0]))
    mate = lax.ppermute(base, "tp", SWAP)

    size = block.shape[0] // 2
    down, up = pl.pallas_call(
        split_kernel,
        out_shape=(
            jax.ShapeDtypeStruct((len(PLANES[0]), size, cols), jnp.bfloat16),
            jax.ShapeDtypeStruct((size, cols), jnp.bfloat16),
        ),
        in_specs=[VMEM],
        out_specs=(VMEM, VMEM),
        name="split",
        compiler_params=ROOM,
    )(block)
    down, up = lax.optimization_barrier((down, up))
    ups = [lax.ppermute(up, ("fsdp", "tp"), relay(part)) for part in range(2)]
    own = lax.all_to_all(down, ("fsdp", "tp"), 0, 0, axis_index_groups=PLANES)
    own, copies, *ups = lax.optimization_barrier((own, copies, *ups))
    x = spread(copies)
    other = lax.ppermute(own, "tp", SWAP)
    ups = lax.all_gather(jnp.stack(ups), "tp", axis=0, axis_index_groups=PAIRS)
    f = lax.axis_index("fsdp")
    place = jnp.stack([core, f // 16, f % 16])
    weights, merged = pl.pallas_call(
        merge_kernel,
        out_shape=(
            jax.ShapeDtypeStruct((tp, cols, 2 * cols), jnp.bfloat16),
            jax.ShapeDtypeStruct((tp * cols, cols), jnp.bfloat16),
        ),
        in_specs=[SMEM] + [VMEM] * 3 + [HBM] * 2,
        out_specs=(HBM, HBM),
        scratch_shapes=[
            pltpu.VMEM((2, 2, cols // 2, cols), jnp.bfloat16),
            pltpu.VMEM((2, tp * cols, cols), jnp.bfloat16),
            pltpu.VMEM((tp * cols, cols), jnp.bfloat16),
            pltpu.VMEM((tp, cols, 2 * cols), jnp.bfloat16),
            pltpu.VMEM((tp, cols, cols), jnp.bfloat16),
            pltpu.SemaphoreType.DMA((2,)),
            pltpu.SemaphoreType.DMA((2, 4)),
        ],
        name="merge",
        compiler_params=WIDE,
    )(place, own, other, ups, base_weight[0], mate)

    gain = gains[0].reshape(CHIPS, 2, 1, cols)
    gain = jnp.where(core == 0, gain, gain[:, ::-1]).reshape(tp, 1, cols)
    results, gives = [], []
    for step in range(STEPS):
        if step:
            x = spread(jnp.broadcast_to(stream.reshape(1, rows, cols), (CHIPS, rows, cols)))
        stream, give, weights = pl.pallas_call(
            step_kernel if step else first_kernel,
            out_shape=(
                jax.ShapeDtypeStruct((2, half, cols), jnp.bfloat16),
                jax.ShapeDtypeStruct((half, cols), jnp.bfloat16),
                jax.ShapeDtypeStruct(weights.shape, weights.dtype),
            ),
            in_specs=[VMEM, VMEM if step else HBM, VMEM, VMEM],
            out_specs=(VMEM, VMEM, VMEM),
            scratch_shapes=[] if step else [pltpu.SemaphoreType.DMA((CHIPS,))],
            input_output_aliases={1: 2} if step else {},
            name="step" if step else "first",
            compiler_params=ROOM if step else pltpu.CompilerParams(vmem_limit_bytes=46 * 1024 * 1024),
        )(x, weights, gain, stream)
        results.append(stream)
        gives.append(give)

    swapped = lax.ppermute(jnp.stack(gives), "tp", SWAP)
    ends = pl.pallas_call(
        finish_kernel,
        out_shape=jax.ShapeDtypeStruct((STEPS, rows, cols), jnp.bfloat16),
        in_specs=[SMEM] + [VMEM] * (STEPS + 1),
        out_specs=VMEM,
        name="finish",
        compiler_params=ROOM,
    )(core[None], swapped, *results)
    return ends, merged[None]


def solution(mesh):
    placed = (
        P("fsdp", "tp"),
        P(None, None, "tp"),
        P(None, "fsdp", None),
        P(None, "fsdp", None),
        P(None, "fsdp", None),
        P(None, "fsdp", None),
        P(),
    )
    return jax.shard_map(
        shards,
        mesh=mesh,
        in_specs=placed,
        out_specs=(P(None, "fsdp", "tp"), P(None, None, "tp")),
        check_vma=False,
    )
```

```python
import jax
import jax.numpy as jnp
from jax import lax
from jax.experimental import pallas as pl
from jax.experimental.pallas import tpu as pltpu
from jax.sharding import PartitionSpec as P

STEPS = 4
CHIPS = 8
GROUPS = [[2 * chip + core for chip in range(CHIPS)] for core in range(2)]
PAIRS = [[2 * chip, 2 * chip + 1] for chip in range(CHIPS)]
SWAP = [(i, i ^ 1) for i in range(2 * CHIPS)]
PLANES = [
    [(16 * (y % 2) + z) * 16 + 8 * (y // 2) + 2 * x + core for y in range(4) for x in range(4)]
    for z in range(16)
    for core in range(2)
]
SHIFTED = [
    ((16 * low + z) * 16 + t, (16 * low + (z + t // 2 + 8 * (t % 2)) % 16) * 16 + t)
    for low in range(2)
    for z in range(16)
    for t in range(16)
]


def relay(part):
    pairs = []
    for z in range(16):
        for low in range(2):
            for block in range(16):
                shift = (z - block) % 16
                source = (16 * low + z) * 16 + 2 * (shift % 8) + shift // 8
                target = 16 * ((block % 4 // 2) ^ part) + z
                pairs.append((source, target * 16 + 8 * low + 2 * (block // 4) + block % 2))
    return pairs


VMEM = pl.BlockSpec(memory_space=pltpu.VMEM)
SMEM = pl.BlockSpec(memory_space=pltpu.SMEM)
HBM = pl.BlockSpec(memory_space=pltpu.HBM)
WIDE = pltpu.CompilerParams(vmem_limit_bytes=51 * 1024 * 1024)
ROOM = pltpu.CompilerParams(vmem_limit_bytes=16 * 1024 * 1024)


def spread(blocks):
    return lax.all_to_all(blocks, "tp", 0, 0, axis_index_groups=GROUPS)


def block_kernel(a_new_ref, a_old_ref, b_new_ref, b_old_ref, out_ref, a_ref, b_ref, sems):
    copies = [
        pltpu.make_async_copy(source, target, sems.at[i])
        for i, (source, target) in enumerate(
            ((a_new_ref, a_ref.at[0]), (a_old_ref, a_ref.at[1]), (b_new_ref, b_ref.at[0]), (b_old_ref, b_ref.at[1]))
        )
    ]
    for copy in copies:
        copy.start()
    for copy in copies:
        copy.wait()
    half, cols = out_ref.shape[0] // 2, out_ref.shape[1]
    new = a_ref[0, 0].astype(jnp.float32)
    old = a_ref[1, 0].astype(jnp.float32)
    slices = []
    for i in range(new.shape[1] // cols):
        slices += [new[:, i * cols : (i + 1) * cols], old[:, i * cols : (i + 1) * cols]]
    out_ref[:half, :] = jnp.concatenate(slices, 0).astype(jnp.bfloat16)
    out_ref[half:, :] = jnp.concatenate([b_ref[0, 0], -b_ref[1, 0]], 1)


def split_kernel(block_ref, down_ref, up_ref):
    half = up_ref.shape[0]
    for chip in range(down_ref.shape[0]):
        down_ref[chip] = block_ref[:half, :]
    up_ref[...] = block_ref[half:, :]


def merge_kernel(
    place_ref, own_ref, other_ref, ups_ref, base_ref, mate_ref, weight_ref, merged_ref, up_ref, old_ref, new_ref, out_ref, in_sems, out_sems
):
    core, low, z = place_ref[0], place_ref[1], place_ref[2]
    cols = base_ref.shape[1]
    span = 2 * cols
    loads = []
    for pair in range(CHIPS):
        rows = slice(pair * span, (pair + 1) * span)
        loads.append(
            [
                pltpu.make_async_copy(ref.at[rows], old_ref.at[i, rows], in_sems.at[i, pair])
                for i, ref in enumerate((base_ref, mate_ref))
            ]
        )
        for load in loads[-1]:
            load.start()
    stores = []
    for left in range(2):
        for part in range(2):
            up_ref[lax.rem(part + low + core, 2), left] = ups_ref[left, part]
    goes = lax.broadcasted_iota(jnp.int32, (cols, cols), 0)
    comes = lax.broadcasted_iota(jnp.int32, (cols, cols), 1)
    chip = comes // 8 % 16
    shift = chip // 8 * 4 + chip % 4 + 8 * ((comes // 128 + core) % 2)
    block = chip // 4 % 2 * 16 + (z + 32 - shift) % 16
    place = comes // 4 % 2 * 128 + block * 4 + comes % 4
    order = jnp.where(place == goes, 1.0, 0.0).astype(jnp.bfloat16)
    up = jnp.dot(up_ref[...].reshape(2 * cols, cols), order, preferred_element_type=jnp.float32).astype(jnp.bfloat16)
    for pair in range(CHIPS):
        parts = [
            ref[:, 16 * pair : 16 * pair + 16, :].astype(jnp.float32).reshape(16, 2, 8, cols)
            for ref in (own_ref, other_ref)
        ]
        for load in loads[pair]:
            load.wait()
        for right in range(2):
            down = jnp.concatenate([part[:, right].reshape(128, cols) for part in parts], 0)
            down = down.astype(jnp.bfloat16).T
            delta = lax.dot_general(down, up, (((1,), (1,)), ((), ())), preferred_element_type=jnp.float32)
            t = 2 * pair + right
            rows = slice(t * cols, (t + 1) * cols)
            mine = (old_ref[0, rows, :].astype(jnp.float32) + delta[:, :cols]).astype(jnp.bfloat16)
            theirs = (old_ref[1, rows, :].astype(jnp.float32) + delta[:, cols:]).astype(jnp.bfloat16)
            new_ref[rows, :] = mine
            which = 2 * pair + lax.rem(right + core, 2)
            out_ref[which, :, :cols] = mine
            out_ref[which, :, cols:] = theirs
        rows, both = slice(pair * span, (pair + 1) * span), slice(2 * pair, 2 * pair + 2)
        stores.append(pltpu.make_async_copy(new_ref.at[rows], merged_ref.at[rows], out_sems.at[0, pair]))
        stores.append(pltpu.make_async_copy(out_ref.at[both], weight_ref.at[both], out_sems.at[1, pair]))
        for store in stores[-2:]:
            store.start()
    for store in stores:
        store.wait()


def decode(x_ref, weight_ref, gain_ref, mine_ref, out_ref, give_ref, arrive):
    _, rows, cols = mine_ref.shape
    blocks = weight_ref.shape[0]
    part = lambda i: x_ref[i // 2, (i % 2) * rows : (i % 2 + 1) * rows, :].astype(jnp.float32)
    squares = part(0) * part(0)
    for i in range(1, blocks):
        squares += part(i) * part(i)
    mean = jnp.sum(squares, axis=1, keepdims=True) / (blocks * cols)
    scale = lax.rsqrt(mean + 1e-06)
    normed = [(part(i) * scale * gain_ref[i]).astype(jnp.bfloat16) for i in range(blocks)]
    total = jnp.zeros((rows, 2 * cols), jnp.float32)
    for i in range(blocks):
        arrive(i)
        total += jnp.dot(normed[i], weight_ref[i], preferred_element_type=jnp.float32)
    for half in range(2):
        branch = total[:, half * cols : (half + 1) * cols]
        out_ref[half] = (mine_ref[half].astype(jnp.float32) + branch).astype(jnp.bfloat16)
    give_ref[...] = out_ref[1]


def first_kernel(x_ref, stored_ref, gain_ref, mine_ref, out_ref, give_ref, weight_ref, sems):
    loads = [
        pltpu.make_async_copy(stored_ref.at[2 * i : 2 * i + 2], weight_ref.at[2 * i : 2 * i + 2], sems.at[i])
        for i in range(CHIPS)
    ]
    for load in loads:
        load.start()

    def arrive(i):
        if i % 2 == 0:
            loads[i // 2].wait()

    decode(x_ref, weight_ref, gain_ref, mine_ref, out_ref, give_ref, arrive)


def step_kernel(x_ref, weight_ref, gain_ref, mine_ref, out_ref, give_ref, _):
    decode(x_ref, weight_ref, gain_ref, mine_ref, out_ref, give_ref, lambda i: None)


def finish_kernel(core_ref, swapped_ref, *refs):
    core = core_ref[0]
    out_ref = refs[-1]
    half = swapped_ref.shape[1]
    mine = pl.ds(pl.multiple_of(core * half, half), half)
    theirs = pl.ds(pl.multiple_of((1 - core) * half, half), half)
    for step in range(STEPS):
        out_ref[step, mine, :] = refs[step][0]
        out_ref[step, theirs, :] = swapped_ref[step]


def shards(tokens, base_weight, a_old, a_new, b_old, b_new, gains):
    rows, cols = tokens.shape
    tp = lax.axis_size("tp")
    t = lax.axis_index("tp")
    core = lax.rem(t, 2)
    half = rows // 2

    block = pl.pallas_call(
        block_kernel,
        out_shape=jax.ShapeDtypeStruct((2 * b_old.shape[1], cols), jnp.bfloat16),
        in_specs=[HBM] * 4,
        out_specs=VMEM,
        scratch_shapes=[
            pltpu.VMEM((2,) + a_new.shape, jnp.bfloat16),
            pltpu.VMEM((2,) + b_new.shape, jnp.bfloat16),
            pltpu.SemaphoreType.DMA((4,)),
        ],
        name="block",
    )(a_new, a_old, b_new, b_old)
    block, tokens = lax.optimization_barrier((block, tokens))
    block = lax.ppermute(block, ("fsdp", "tp"), SHIFTED)

    both = lax.all_gather(tokens, "tp", axis=0, axis_index_groups=PAIRS)
    both = lax.dynamic_slice_in_dim(both, core * half, half, 1)
    stream = jnp.where(core == 0, both, both[::-1])
    copies = jnp.broadcast_to(stream.reshape(1, rows, cols), (CHIPS, rows, cols))
    copies, base = lax.optimization_barrier((copies, base_weight[0]))
    mate = lax.ppermute(base, "tp", SWAP)

    size = block.shape[0] // 2
    down, up = pl.pallas_call(
        split_kernel,
        out_shape=(
            jax.ShapeDtypeStruct((len(PLANES[0]), size, cols), jnp.bfloat16),
            jax.ShapeDtypeStruct((size, cols), jnp.bfloat16),
        ),
        in_specs=[VMEM],
        out_specs=(VMEM, VMEM),
        name="split",
        compiler_params=ROOM,
    )(block)
    down, up = lax.optimization_barrier((down, up))
    ups = [lax.ppermute(up, ("fsdp", "tp"), relay(part)) for part in range(2)]
    own = lax.all_to_all(down, ("fsdp", "tp"), 0, 0, axis_index_groups=PLANES)
    own, copies, *ups = lax.optimization_barrier((own, copies, *ups))
    x = spread(copies)
    other = lax.ppermute(own, "tp", SWAP)
    ups = lax.all_gather(jnp.stack(ups), "tp", axis=0, axis_index_groups=PAIRS)
    f = lax.axis_index("fsdp")
    place = jnp.stack([core, f // 16, f % 16])
    weights, merged = pl.pallas_call(
        merge_kernel,
        out_shape=(
            jax.ShapeDtypeStruct((tp, cols, 2 * cols), jnp.bfloat16),
            jax.ShapeDtypeStruct((tp * cols, cols), jnp.bfloat16),
        ),
        in_specs=[SMEM] + [VMEM] * 3 + [HBM] * 2,
        out_specs=(HBM, HBM),
        scratch_shapes=[
            pltpu.VMEM((2, 2, cols // 2, cols), jnp.bfloat16),
            pltpu.VMEM((2, tp * cols, cols), jnp.bfloat16),
            pltpu.VMEM((tp * cols, cols), jnp.bfloat16),
            pltpu.VMEM((tp, cols, 2 * cols), jnp.bfloat16),
            pltpu.SemaphoreType.DMA((2, CHIPS)),
            pltpu.SemaphoreType.DMA((2, CHIPS)),
        ],
        name="merge",
        compiler_params=WIDE,
    )(place, own, other, ups, base_weight[0], mate)

    gain = gains[0].reshape(CHIPS, 2, 1, cols)
    gain = jnp.where(core == 0, gain, gain[:, ::-1]).reshape(tp, 1, cols)
    results, gives = [], []
    for step in range(STEPS):
        if step:
            x = spread(jnp.broadcast_to(stream.reshape(1, rows, cols), (CHIPS, rows, cols)))
        stream, give, weights = pl.pallas_call(
            step_kernel if step else first_kernel,
            out_shape=(
                jax.ShapeDtypeStruct((2, half, cols), jnp.bfloat16),
                jax.ShapeDtypeStruct((half, cols), jnp.bfloat16),
                jax.ShapeDtypeStruct(weights.shape, weights.dtype),
            ),
            in_specs=[VMEM, VMEM if step else HBM, VMEM, VMEM],
            out_specs=(VMEM, VMEM, VMEM),
            scratch_shapes=[] if step else [pltpu.SemaphoreType.DMA((CHIPS,))],
            input_output_aliases={1: 2} if step else {},
            name="step" if step else "first",
            compiler_params=ROOM if step else pltpu.CompilerParams(vmem_limit_bytes=46 * 1024 * 1024),
        )(x, weights, gain, stream)
        results.append(stream)
        gives.append(give)

    swapped = lax.ppermute(jnp.stack(gives), "tp", SWAP)
    ends = pl.pallas_call(
        finish_kernel,
        out_shape=jax.ShapeDtypeStruct((STEPS, rows, cols), jnp.bfloat16),
        in_specs=[SMEM] + [VMEM] * (STEPS + 1),
        out_specs=VMEM,
        name="finish",
        compiler_params=ROOM,
    )(core[None], swapped, *results)
    return ends, merged[None]


def solution(mesh):
    placed = (
        P("fsdp", "tp"),
        P(None, None, "tp"),
        P(None, "fsdp", None),
        P(None, "fsdp", None),
        P(None, "fsdp", None),
        P(None, "fsdp", None),
        P(),
    )
    return jax.shard_map(
        shards,
        mesh=mesh,
        in_specs=placed,
        out_specs=(P(None, "fsdp", "tp"), P(None, None, "tp")),
        check_vma=False,
    )
```

```python
import jax
import jax.numpy as jnp
from jax import lax
from jax.experimental import pallas as pl
from jax.experimental.pallas import tpu as pltpu
from jax.sharding import PartitionSpec as P

STEPS = 4
CHIPS = 8
GROUPS = [[2 * chip + core for chip in range(CHIPS)] for core in range(2)]
PAIRS = [[2 * chip, 2 * chip + 1] for chip in range(CHIPS)]
SWAP = [(i, i ^ 1) for i in range(2 * CHIPS)]
PLANES = [
    [(16 * (y % 2) + z) * 16 + 8 * (y // 2) + 2 * x + core for y in range(4) for x in range(4)]
    for z in range(16)
    for core in range(2)
]
SHIFTED = [
    ((16 * low + z) * 16 + t, (16 * low + (z + t // 2 + 8 * (t % 2)) % 16) * 16 + t)
    for low in range(2)
    for z in range(16)
    for t in range(16)
]


def relay(part):
    pairs = []
    for z in range(16):
        for low in range(2):
            for block in range(16):
                shift = (z - block) % 16
                source = (16 * low + z) * 16 + 2 * (shift % 8) + shift // 8
                target = 16 * ((block % 4 // 2) ^ part) + z
                pairs.append((source, target * 16 + 8 * low + 2 * (block // 4) + block % 2))
    return pairs


VMEM = pl.BlockSpec(memory_space=pltpu.VMEM)
SMEM = pl.BlockSpec(memory_space=pltpu.SMEM)
HBM = pl.BlockSpec(memory_space=pltpu.HBM)
WIDE = pltpu.CompilerParams(vmem_limit_bytes=51 * 1024 * 1024)
ROOM = pltpu.CompilerParams(vmem_limit_bytes=16 * 1024 * 1024)


def spread(blocks):
    return lax.all_to_all(blocks, "tp", 0, 0, axis_index_groups=GROUPS)


def block_kernel(a_new_ref, a_old_ref, b_new_ref, b_old_ref, out_ref, a_ref, b_ref, sems):
    copies = [
        pltpu.make_async_copy(source, target, sems.at[i])
        for i, (source, target) in enumerate(
            ((a_new_ref, a_ref.at[0]), (a_old_ref, a_ref.at[1]), (b_new_ref, b_ref.at[0]), (b_old_ref, b_ref.at[1]))
        )
    ]
    for copy in copies:
        copy.start()
    for copy in copies:
        copy.wait()
    half, cols = out_ref.shape[0] // 2, out_ref.shape[1]
    new = a_ref[0, 0].astype(jnp.float32)
    old = a_ref[1, 0].astype(jnp.float32)
    slices = []
    for i in range(new.shape[1] // cols):
        slices += [new[:, i * cols : (i + 1) * cols], old[:, i * cols : (i + 1) * cols]]
    out_ref[:half, :] = jnp.concatenate(slices, 0).astype(jnp.bfloat16)
    out_ref[half:, :] = jnp.concatenate([b_ref[0, 0], -b_ref[1, 0]], 1)


def split_kernel(block_ref, down_ref, up_ref):
    half = up_ref.shape[0]
    for chip in range(down_ref.shape[0]):
        down_ref[chip] = block_ref[:half, :]
    up_ref[...] = block_ref[half:, :]


def turn_kernel(own_ref, turned_ref):
    cols = own_ref.shape[2]
    for pair in range(CHIPS):
        part = own_ref[:, 16 * pair : 16 * pair + 16, :].astype(jnp.float32).reshape(16, 2, 8, cols)
        for right in range(2):
            turned_ref[2 * pair + right] = part[:, right].reshape(128, cols).astype(jnp.bfloat16).T


def merge_kernel(
    place_ref, own_ref, other_ref, ups_ref, base_ref, mate_ref, weight_ref, merged_ref, up_ref, old_ref, new_ref, out_ref, in_sems, out_sems
):
    core, low, z = place_ref[0], place_ref[1], place_ref[2]
    cols = base_ref.shape[1]
    span = 2 * cols
    loads = []
    for pair in range(CHIPS):
        rows = slice(pair * span, (pair + 1) * span)
        loads.append(
            [
                pltpu.make_async_copy(ref.at[rows], old_ref.at[i, rows], in_sems.at[i, pair])
                for i, ref in enumerate((base_ref, mate_ref))
            ]
        )
        for load in loads[-1]:
            load.start()
    stores = []
    for left in range(2):
        for part in range(2):
            up_ref[lax.rem(part + low + core, 2), left] = ups_ref[left, part]
    goes = lax.broadcasted_iota(jnp.int32, (cols, cols), 0)
    comes = lax.broadcasted_iota(jnp.int32, (cols, cols), 1)
    chip = comes // 8 % 16
    shift = chip // 8 * 4 + chip % 4 + 8 * ((comes // 128 + core) % 2)
    block = chip // 4 % 2 * 16 + (z + 32 - shift) % 16
    place = comes // 4 % 2 * 128 + block * 4 + comes % 4
    order = jnp.where(place == goes, 1.0, 0.0).astype(jnp.bfloat16)
    up = jnp.dot(up_ref[...].reshape(2 * cols, cols), order, preferred_element_type=jnp.float32).astype(jnp.bfloat16)
    for pair in range(CHIPS):
        for load in loads[pair]:
            load.wait()
        for right in range(2):
            t = 2 * pair + right
            down = jnp.concatenate([own_ref[t], other_ref[t]], 1)
            delta = lax.dot_general(down, up, (((1,), (1,)), ((), ())), preferred_element_type=jnp.float32)
            rows = slice(t * cols, (t + 1) * cols)
            mine = (old_ref[0, rows, :].astype(jnp.float32) + delta[:, :cols]).astype(jnp.bfloat16)
            theirs = (old_ref[1, rows, :].astype(jnp.float32) + delta[:, cols:]).astype(jnp.bfloat16)
            new_ref[rows, :] = mine
            which = 2 * pair + lax.rem(right + core, 2)
            out_ref[which, :, :cols] = mine
            out_ref[which, :, cols:] = theirs
        rows, both = slice(pair * span, (pair + 1) * span), slice(2 * pair, 2 * pair + 2)
        stores.append(pltpu.make_async_copy(new_ref.at[rows], merged_ref.at[rows], out_sems.at[0, pair]))
        stores.append(pltpu.make_async_copy(out_ref.at[both], weight_ref.at[both], out_sems.at[1, pair]))
        for store in stores[-2:]:
            store.start()
    for store in stores:
        store.wait()


def decode(x_ref, weight_ref, gain_ref, mine_ref, out_ref, give_ref, arrive):
    _, rows, cols = mine_ref.shape
    blocks = weight_ref.shape[0]
    part = lambda i: x_ref[i // 2, (i % 2) * rows : (i % 2 + 1) * rows, :].astype(jnp.float32)
    squares = part(0) * part(0)
    for i in range(1, blocks):
        squares += part(i) * part(i)
    mean = jnp.sum(squares, axis=1, keepdims=True) / (blocks * cols)
    scale = lax.rsqrt(mean + 1e-06)
    normed = [(part(i) * scale * gain_ref[i]).astype(jnp.bfloat16) for i in range(blocks)]
    total = jnp.zeros((rows, 2 * cols), jnp.float32)
    for i in range(blocks):
        arrive(i)
        total += jnp.dot(normed[i], weight_ref[i], preferred_element_type=jnp.float32)
    for half in range(2):
        branch = total[:, half * cols : (half + 1) * cols]
        out_ref[half] = (mine_ref[half].astype(jnp.float32) + branch).astype(jnp.bfloat16)
    give_ref[...] = out_ref[1]


def first_kernel(x_ref, stored_ref, gain_ref, mine_ref, out_ref, give_ref, weight_ref, sems):
    loads = [
        pltpu.make_async_copy(stored_ref.at[2 * i : 2 * i + 2], weight_ref.at[2 * i : 2 * i + 2], sems.at[i])
        for i in range(CHIPS)
    ]
    for load in loads:
        load.start()

    def arrive(i):
        if i % 2 == 0:
            loads[i // 2].wait()

    decode(x_ref, weight_ref, gain_ref, mine_ref, out_ref, give_ref, arrive)


def step_kernel(x_ref, weight_ref, gain_ref, mine_ref, out_ref, give_ref, _):
    decode(x_ref, weight_ref, gain_ref, mine_ref, out_ref, give_ref, lambda i: None)


def finish_kernel(core_ref, swapped_ref, *refs):
    core = core_ref[0]
    out_ref = refs[-1]
    half = swapped_ref.shape[1]
    mine = pl.ds(pl.multiple_of(core * half, half), half)
    theirs = pl.ds(pl.multiple_of((1 - core) * half, half), half)
    for step in range(STEPS):
        out_ref[step, mine, :] = refs[step][0]
        out_ref[step, theirs, :] = swapped_ref[step]


def shards(tokens, base_weight, a_old, a_new, b_old, b_new, gains):
    rows, cols = tokens.shape
    tp = lax.axis_size("tp")
    t = lax.axis_index("tp")
    core = lax.rem(t, 2)
    half = rows // 2

    block = pl.pallas_call(
        block_kernel,
        out_shape=jax.ShapeDtypeStruct((2 * b_old.shape[1], cols), jnp.bfloat16),
        in_specs=[HBM] * 4,
        out_specs=VMEM,
        scratch_shapes=[
            pltpu.VMEM((2,) + a_new.shape, jnp.bfloat16),
            pltpu.VMEM((2,) + b_new.shape, jnp.bfloat16),
            pltpu.SemaphoreType.DMA((4,)),
        ],
        name="block",
    )(a_new, a_old, b_new, b_old)
    block, tokens = lax.optimization_barrier((block, tokens))
    block = lax.ppermute(block, ("fsdp", "tp"), SHIFTED)

    both = lax.all_gather(tokens, "tp", axis=0, axis_index_groups=PAIRS)
    both = lax.dynamic_slice_in_dim(both, core * half, half, 1)
    stream = jnp.where(core == 0, both, both[::-1])
    copies = jnp.broadcast_to(stream.reshape(1, rows, cols), (CHIPS, rows, cols))
    copies, base = lax.optimization_barrier((copies, base_weight[0]))
    mate = lax.ppermute(base, "tp", SWAP)

    size = block.shape[0] // 2
    down, up = pl.pallas_call(
        split_kernel,
        out_shape=(
            jax.ShapeDtypeStruct((len(PLANES[0]), size, cols), jnp.bfloat16),
            jax.ShapeDtypeStruct((size, cols), jnp.bfloat16),
        ),
        in_specs=[VMEM],
        out_specs=(VMEM, VMEM),
        name="split",
        compiler_params=ROOM,
    )(block)
    down, up = lax.optimization_barrier((down, up))
    ups = [lax.ppermute(up, ("fsdp", "tp"), relay(part)) for part in range(2)]
    own = lax.all_to_all(down, ("fsdp", "tp"), 0, 0, axis_index_groups=PLANES)
    own, copies, *ups = lax.optimization_barrier((own, copies, *ups))
    x = spread(copies)
    own = pl.pallas_call(
        turn_kernel,
        out_shape=jax.ShapeDtypeStruct((tp, cols, size), jnp.bfloat16),
        in_specs=[VMEM],
        out_specs=VMEM,
        name="turn",
        compiler_params=ROOM,
    )(own)
    other = lax.ppermute(own, "tp", SWAP)
    ups = lax.all_gather(jnp.stack(ups), "tp", axis=0, axis_index_groups=PAIRS)
    f = lax.axis_index("fsdp")
    place = jnp.stack([core, f // 16, f % 16])
    weights, merged = pl.pallas_call(
        merge_kernel,
        out_shape=(
            jax.ShapeDtypeStruct((tp, cols, 2 * cols), jnp.bfloat16),
            jax.ShapeDtypeStruct((tp * cols, cols), jnp.bfloat16),
        ),
        in_specs=[SMEM] + [VMEM] * 3 + [HBM] * 2,
        out_specs=(HBM, HBM),
        scratch_shapes=[
            pltpu.VMEM((2, 2, cols // 2, cols), jnp.bfloat16),
            pltpu.VMEM((2, tp * cols, cols), jnp.bfloat16),
            pltpu.VMEM((tp * cols, cols), jnp.bfloat16),
            pltpu.VMEM((tp, cols, 2 * cols), jnp.bfloat16),
            pltpu.SemaphoreType.DMA((2, CHIPS)),
            pltpu.SemaphoreType.DMA((2, CHIPS)),
        ],
        name="merge",
        compiler_params=WIDE,
    )(place, own, other, ups, base_weight[0], mate)

    gain = gains[0].reshape(CHIPS, 2, 1, cols)
    gain = jnp.where(core == 0, gain, gain[:, ::-1]).reshape(tp, 1, cols)
    results, gives = [], []
    for step in range(STEPS):
        if step:
            x = spread(jnp.broadcast_to(stream.reshape(1, rows, cols), (CHIPS, rows, cols)))
        stream, give, weights = pl.pallas_call(
            step_kernel if step else first_kernel,
            out_shape=(
                jax.ShapeDtypeStruct((2, half, cols), jnp.bfloat16),
                jax.ShapeDtypeStruct((half, cols), jnp.bfloat16),
                jax.ShapeDtypeStruct(weights.shape, weights.dtype),
            ),
            in_specs=[VMEM, VMEM if step else HBM, VMEM, VMEM],
            out_specs=(VMEM, VMEM, VMEM),
            scratch_shapes=[] if step else [pltpu.SemaphoreType.DMA((CHIPS,))],
            input_output_aliases={1: 2} if step else {},
            name="step" if step else "first",
            compiler_params=ROOM if step else pltpu.CompilerParams(vmem_limit_bytes=46 * 1024 * 1024),
        )(x, weights, gain, stream)
        results.append(stream)
        gives.append(give)

    swapped = lax.ppermute(jnp.stack(gives), "tp", SWAP)
    ends = pl.pallas_call(
        finish_kernel,
        out_shape=jax.ShapeDtypeStruct((STEPS, rows, cols), jnp.bfloat16),
        in_specs=[SMEM] + [VMEM] * (STEPS + 1),
        out_specs=VMEM,
        name="finish",
        compiler_params=ROOM,
    )(core[None], swapped, *results)
    return ends, merged[None]


def solution(mesh):
    placed = (
        P("fsdp", "tp"),
        P(None, None, "tp"),
        P(None, "fsdp", None),
        P(None, "fsdp", None),
        P(None, "fsdp", None),
        P(None, "fsdp", None),
        P(),
    )
    return jax.shard_map(
        shards,
        mesh=mesh,
        in_specs=placed,
        out_specs=(P(None, "fsdp", "tp"), P(None, None, "tp")),
        check_vma=False,
    )
```

```python
import jax
import jax.numpy as jnp
from jax import lax
from jax.experimental import pallas as pl
from jax.experimental.pallas import tpu as pltpu
from jax.sharding import PartitionSpec as P

STEPS = 4
CHIPS = 8
GROUPS = [[2 * chip + core for chip in range(CHIPS)] for core in range(2)]
PAIRS = [[2 * chip, 2 * chip + 1] for chip in range(CHIPS)]
SWAP = [(i, i ^ 1) for i in range(2 * CHIPS)]
PLANES = [
    [(16 * (y % 2) + z) * 16 + 8 * (y // 2) + 2 * x + core for y in range(4) for x in range(4)]
    for z in range(16)
    for core in range(2)
]
SHIFTED = [
    ((16 * low + z) * 16 + t, (16 * low + (z + t // 2 + 8 * (t % 2)) % 16) * 16 + t)
    for low in range(2)
    for z in range(16)
    for t in range(16)
]


def relay(part):
    pairs = []
    for z in range(16):
        for low in range(2):
            for block in range(16):
                shift = (z - block) % 16
                source = (16 * low + z) * 16 + 2 * (shift % 8) + shift // 8
                target = 16 * ((block % 4 // 2) ^ part) + z
                pairs.append((source, target * 16 + 8 * low + 2 * (block // 4) + block % 2))
    return pairs


VMEM = pl.BlockSpec(memory_space=pltpu.VMEM)
SMEM = pl.BlockSpec(memory_space=pltpu.SMEM)
HBM = pl.BlockSpec(memory_space=pltpu.HBM)
WIDE = pltpu.CompilerParams(vmem_limit_bytes=51 * 1024 * 1024)
ROOM = pltpu.CompilerParams(vmem_limit_bytes=16 * 1024 * 1024)


def spread(blocks):
    return lax.all_to_all(blocks, "tp", 0, 0, axis_index_groups=GROUPS)


def block_kernel(a_new_ref, a_old_ref, b_new_ref, b_old_ref, out_ref, a_ref, b_ref, sems):
    copies = [
        pltpu.make_async_copy(source, target, sems.at[i])
        for i, (source, target) in enumerate(
            ((a_new_ref, a_ref.at[0]), (a_old_ref, a_ref.at[1]), (b_new_ref, b_ref.at[0]), (b_old_ref, b_ref.at[1]))
        )
    ]
    for copy in copies:
        copy.start()
    for copy in copies:
        copy.wait()
    half, cols = out_ref.shape[0] // 2, out_ref.shape[1]
    new = a_ref[0, 0].astype(jnp.float32)
    old = a_ref[1, 0].astype(jnp.float32)
    slices = []
    for i in range(new.shape[1] // cols):
        slices += [new[:, i * cols : (i + 1) * cols], old[:, i * cols : (i + 1) * cols]]
    out_ref[:half, :] = jnp.concatenate(slices, 0).astype(jnp.bfloat16)
    out_ref[half:, :] = jnp.concatenate([b_ref[0, 0], -b_ref[1, 0]], 1)


def split_kernel(block_ref, down_ref, up_ref):
    half = up_ref.shape[0]
    for chip in range(down_ref.shape[0]):
        down_ref[chip] = block_ref[:half, :]
    up_ref[...] = block_ref[half:, :]


def merge_kernel(
    place_ref, own_ref, other_ref, ups_ref, base_ref, mate_ref, weight_ref, merged_ref, up_ref, old_ref, new_ref, out_ref, in_sems, out_sems
):
    core, low, z = place_ref[0], place_ref[1], place_ref[2]
    cols = base_ref.shape[1]
    span = 2 * cols
    loads = []
    for pair in range(CHIPS):
        rows = slice(pair * span, (pair + 1) * span)
        loads.append(
            [
                pltpu.make_async_copy(ref.at[rows], old_ref.at[i, rows], in_sems.at[i, pair])
                for i, ref in enumerate((base_ref, mate_ref))
            ]
        )
        for load in loads[-1]:
            load.start()
    stores = []
    for left in range(2):
        for part in range(2):
            up_ref[lax.rem(part + low + core, 2), left] = ups_ref[left, part]
    goes = lax.broadcasted_iota(jnp.int32, (cols, cols), 0)
    comes = lax.broadcasted_iota(jnp.int32, (cols, cols), 1)
    chip = comes // 8 % 16
    shift = chip // 8 * 4 + chip % 4 + 8 * ((comes // 128 + core) % 2)
    block = chip // 4 % 2 * 16 + (z + 32 - shift) % 16
    place = comes // 4 % 2 * 128 + block * 4 + comes % 4
    order = jnp.where(place == goes, 1.0, 0.0).astype(jnp.bfloat16)
    up = jnp.dot(up_ref[...].reshape(2 * cols, cols), order, preferred_element_type=jnp.float32).astype(jnp.bfloat16)
    for pair in range(CHIPS):
        parts = [
            ref[:, 16 * pair : 16 * pair + 16, :].astype(jnp.float32).reshape(16, 2, 8, cols)
            for ref in (own_ref, other_ref)
        ]
        for load in loads[pair]:
            load.wait()
        for right in range(2):
            down = jnp.concatenate([part[:, right].reshape(128, cols) for part in parts], 0)
            down = down.astype(jnp.bfloat16).T
            delta = lax.dot_general(down, up, (((1,), (1,)), ((), ())), preferred_element_type=jnp.float32)
            t = 2 * pair + right
            rows = slice(t * cols, (t + 1) * cols)
            mine = (old_ref[0, rows, :].astype(jnp.float32) + delta[:, :cols]).astype(jnp.bfloat16)
            theirs = (old_ref[1, rows, :].astype(jnp.float32) + delta[:, cols:]).astype(jnp.bfloat16)
            new_ref[rows, :] = mine
            which = 2 * pair + lax.rem(right + core, 2)
            out_ref[which, :, :cols] = mine
            out_ref[which, :, cols:] = theirs
        rows, both = slice(pair * span, (pair + 1) * span), slice(2 * pair, 2 * pair + 2)
        stores.append(pltpu.make_async_copy(new_ref.at[rows], merged_ref.at[rows], out_sems.at[0, pair]))
        stores.append(pltpu.make_async_copy(out_ref.at[both], weight_ref.at[both], out_sems.at[1, pair]))
        for store in stores[-2:]:
            store.start()
    for store in stores:
        store.wait()


def decode(x_ref, weight_ref, gain_ref, mine_ref, out_ref, give_ref, arrive):
    _, rows, cols = mine_ref.shape
    blocks = weight_ref.shape[0]
    part = lambda i: x_ref[i // 2, (i % 2) * rows : (i % 2 + 1) * rows, :].astype(jnp.float32)
    squares = part(0) * part(0)
    for i in range(1, blocks):
        squares += part(i) * part(i)
    mean = jnp.sum(squares, axis=1, keepdims=True) / (blocks * cols)
    scale = lax.rsqrt(mean + 1e-06)
    normed = [(part(i) * scale * gain_ref[i]).astype(jnp.bfloat16) for i in range(blocks)]
    total = jnp.zeros((rows, 2 * cols), jnp.float32)
    for i in range(blocks):
        arrive(i)
        total += jnp.dot(normed[i], weight_ref[i], preferred_element_type=jnp.float32)
    for half in range(2):
        branch = total[:, half * cols : (half + 1) * cols]
        out_ref[half] = (mine_ref[half].astype(jnp.float32) + branch).astype(jnp.bfloat16)
    give_ref[...] = out_ref[1]


def first_kernel(x_ref, stored_ref, gain_ref, mine_ref, out_ref, give_ref, weight_ref, sems):
    loads = [
        pltpu.make_async_copy(stored_ref.at[4 * i : 4 * i + 4], weight_ref.at[4 * i : 4 * i + 4], sems.at[i])
        for i in range(CHIPS // 2)
    ]
    for load in loads:
        load.start()

    def arrive(i):
        if i % 4 == 0:
            loads[i // 4].wait()

    decode(x_ref, weight_ref, gain_ref, mine_ref, out_ref, give_ref, arrive)


def step_kernel(x_ref, weight_ref, gain_ref, mine_ref, out_ref, give_ref, _):
    decode(x_ref, weight_ref, gain_ref, mine_ref, out_ref, give_ref, lambda i: None)


def finish_kernel(core_ref, swapped_ref, *refs):
    core = core_ref[0]
    out_ref = refs[-1]
    half = swapped_ref.shape[1]
    mine = pl.ds(pl.multiple_of(core * half, half), half)
    theirs = pl.ds(pl.multiple_of((1 - core) * half, half), half)
    for step in range(STEPS):
        out_ref[step, mine, :] = refs[step][0]
        out_ref[step, theirs, :] = swapped_ref[step]


def shards(tokens, base_weight, a_old, a_new, b_old, b_new, gains):
    rows, cols = tokens.shape
    tp = lax.axis_size("tp")
    t = lax.axis_index("tp")
    core = lax.rem(t, 2)
    half = rows // 2

    block = pl.pallas_call(
        block_kernel,
        out_shape=jax.ShapeDtypeStruct((2 * b_old.shape[1], cols), jnp.bfloat16),
        in_specs=[HBM] * 4,
        out_specs=VMEM,
        scratch_shapes=[
            pltpu.VMEM((2,) + a_new.shape, jnp.bfloat16),
            pltpu.VMEM((2,) + b_new.shape, jnp.bfloat16),
            pltpu.SemaphoreType.DMA((4,)),
        ],
        name="block",
    )(a_new, a_old, b_new, b_old)
    block, tokens = lax.optimization_barrier((block, tokens))
    block = lax.ppermute(block, ("fsdp", "tp"), SHIFTED)

    both = lax.all_gather(tokens, "tp", axis=0, axis_index_groups=PAIRS)
    both = lax.dynamic_slice_in_dim(both, core * half, half, 1)
    stream = jnp.where(core == 0, both, both[::-1])
    copies = jnp.broadcast_to(stream.reshape(1, rows, cols), (CHIPS, rows, cols))
    copies, base = lax.optimization_barrier((copies, base_weight[0]))
    mate = lax.ppermute(base, "tp", SWAP)

    size = block.shape[0] // 2
    down, up = pl.pallas_call(
        split_kernel,
        out_shape=(
            jax.ShapeDtypeStruct((len(PLANES[0]), size, cols), jnp.bfloat16),
            jax.ShapeDtypeStruct((size, cols), jnp.bfloat16),
        ),
        in_specs=[VMEM],
        out_specs=(VMEM, VMEM),
        name="split",
        compiler_params=ROOM,
    )(block)
    down, up = lax.optimization_barrier((down, up))
    ups = [lax.ppermute(up, ("fsdp", "tp"), relay(part)) for part in range(2)]
    own = lax.all_to_all(down, ("fsdp", "tp"), 0, 0, axis_index_groups=PLANES)
    own, copies, *ups = lax.optimization_barrier((own, copies, *ups))
    x = spread(copies)
    other = lax.ppermute(own, "tp", SWAP)
    ups = lax.all_gather(jnp.stack(ups), "tp", axis=0, axis_index_groups=PAIRS)
    f = lax.axis_index("fsdp")
    place = jnp.stack([core, f // 16, f % 16])
    weights, merged = pl.pallas_call(
        merge_kernel,
        out_shape=(
            jax.ShapeDtypeStruct((tp, cols, 2 * cols), jnp.bfloat16),
            jax.ShapeDtypeStruct((tp * cols, cols), jnp.bfloat16),
        ),
        in_specs=[SMEM] + [VMEM] * 3 + [HBM] * 2,
        out_specs=(HBM, HBM),
        scratch_shapes=[
            pltpu.VMEM((2, 2, cols // 2, cols), jnp.bfloat16),
            pltpu.VMEM((2, tp * cols, cols), jnp.bfloat16),
            pltpu.VMEM((tp * cols, cols), jnp.bfloat16),
            pltpu.VMEM((tp, cols, 2 * cols), jnp.bfloat16),
            pltpu.SemaphoreType.DMA((2, CHIPS)),
            pltpu.SemaphoreType.DMA((2, CHIPS)),
        ],
        name="merge",
        compiler_params=WIDE,
    )(place, own, other, ups, base_weight[0], mate)

    gain = gains[0].reshape(CHIPS, 2, 1, cols)
    gain = jnp.where(core == 0, gain, gain[:, ::-1]).reshape(tp, 1, cols)
    results, gives = [], []
    for step in range(STEPS):
        if step:
            x = spread(jnp.broadcast_to(stream.reshape(1, rows, cols), (CHIPS, rows, cols)))
        stream, give, weights = pl.pallas_call(
            step_kernel if step else first_kernel,
            out_shape=(
                jax.ShapeDtypeStruct((2, half, cols), jnp.bfloat16),
                jax.ShapeDtypeStruct((half, cols), jnp.bfloat16),
                jax.ShapeDtypeStruct(weights.shape, weights.dtype),
            ),
            in_specs=[VMEM, VMEM if step else HBM, VMEM, VMEM],
            out_specs=(VMEM, VMEM, VMEM),
            scratch_shapes=[] if step else [pltpu.SemaphoreType.DMA((CHIPS // 2,))],
            input_output_aliases={1: 2} if step else {},
            name="step" if step else "first",
            compiler_params=ROOM if step else pltpu.CompilerParams(vmem_limit_bytes=46 * 1024 * 1024),
        )(x, weights, gain, stream)
        results.append(stream)
        gives.append(give)

    swapped = lax.ppermute(jnp.stack(gives), "tp", SWAP)
    ends = pl.pallas_call(
        finish_kernel,
        out_shape=jax.ShapeDtypeStruct((STEPS, rows, cols), jnp.bfloat16),
        in_specs=[SMEM] + [VMEM] * (STEPS + 1),
        out_specs=VMEM,
        name="finish",
        compiler_params=ROOM,
    )(core[None], swapped, *results)
    return ends, merged[None]


def solution(mesh):
    placed = (
        P("fsdp", "tp"),
        P(None, None, "tp"),
        P(None, "fsdp", None),
        P(None, "fsdp", None),
        P(None, "fsdp", None),
        P(None, "fsdp", None),
        P(),
    )
    return jax.shard_map(
        shards,
        mesh=mesh,
        in_specs=placed,
        out_specs=(P(None, "fsdp", "tp"), P(None, None, "tp")),
        check_vma=False,
    )
```
